128 devices in a mesh: gx: 8 (over x, z_hi), gy: 16 (over y, z_lo, core).
Axes of the slice: x: 4, y: 4, z: 4 (z_hi: 2, z_lo: 2; z = z_hi * 2 + z_lo), core: 2. Of those that a mesh axis runs over, the one named last changes fastest.
Arguments:
- x_embed: bfloat16 [16384, 1024], P(('gx', 'gy')), may hold values from -2 to 2
- y_embed: bfloat16 [16384, 1024], P(('gx', 'gy')), may hold values from -4 to 4
Outputs:
- grad_x: float32 [16384, 1024], P(('gx', 'gy'))
- grad_y: float32 [16384, 1024], P(('gx', 'gy'))
The draws below stay inside these ranges and needn't reach their ends.
All inputs are finite; a program needn't handle non-finite values.
Results may differ from the reference program's by a relative error of at most 0.0003.
Values may be sent and summed in bfloat16 or wider, within the bound.
A program may use at most 128 MiB of HBM per device.

```python
import math
import jax
import jax.numpy as jnp
from jax import lax

D = 1024
ANCHORS = 16384


def shared_base(key):
    first, second = jax.random.split(key)
    base = jnp.clip(jax.random.normal(first, (ANCHORS, D), jnp.float32), -6.0, 6.0)
    scales = jnp.exp(jax.random.uniform(second, (ANCHORS, 1), jnp.float32, math.log(0.3), math.log(3.0)))
    return (base, scales)


def draw_x_embed(key, part):
    base, scales = shared_base(key)
    key = jax.random.fold_in(key, 11)
    col_key = jax.random.fold_in(key, 0)
    columns = jnp.exp(jax.random.uniform(col_key, (1, D), jnp.float32, math.log(0.5), math.log(2.0)))
    return (scales * base * columns / math.sqrt(D)).astype(jnp.bfloat16)


def draw_y_embed(key, part):
    base, scales = shared_base(key)
    key = jax.random.fold_in(key, 23)
    own_key, tilt_key, col_key = jax.random.split(key, 3)
    own = jnp.clip(jax.random.normal(own_key, (ANCHORS, D), jnp.float32), -6.0, 6.0)
    tilt = jnp.exp(jax.random.uniform(tilt_key, (ANCHORS, 1), jnp.float32, math.log(0.5), math.log(2.0)))
    columns = jnp.exp(jax.random.uniform(col_key, (1, D), jnp.float32, math.log(0.5), math.log(2.0)))
    mixed = 0.7 * base + 0.7 * own
    return (scales * tilt * mixed * columns / math.sqrt(D)).astype(jnp.bfloat16)


def setup_inputs(seed: int = 0) -> dict:
    streams_of = jax.random.split(jax.random.key(seed), 3)
    return {
        "x_embed": draw_x_embed(jax.random.fold_in(streams_of[2], 71), 0),
        "y_embed": draw_y_embed(jax.random.fold_in(streams_of[2], 71), 0),
    }


dist_eps = 0.0001

def squares(block):
    wide = block.astype(jnp.float32)
    return lax.optimization_barrier(jnp.sum(wide * wide, axis=1))

def block_terms(x_block, y_block, col_x, col_y, norm_cx, norm_cy):
    gram_x = lax.dot_general(x_block, col_x, (((1,), (1,)), ((), ())), preferred_element_type=jnp.float32)
    gram_y = lax.dot_general(y_block, col_y, (((1,), (1,)), ((), ())), preferred_element_type=jnp.float32)
    dist_x = jnp.sqrt(squares(x_block)[:, None] + norm_cx[None, :] - 2.0 * gram_x + dist_eps)
    dist_y = jnp.sqrt(squares(y_block)[:, None] + norm_cy[None, :] - 2.0 * gram_y + dist_eps)
    differ = dist_x - dist_y
    weight_x = (differ / dist_x).astype(jnp.bfloat16)
    weight_y = (differ / dist_y).astype(jnp.bfloat16)
    term_x = lax.optimization_barrier(jnp.sum(weight_x.astype(jnp.float32), axis=1))[:, None] * x_block.astype(jnp.float32) - jnp.dot(weight_x, col_x, preferred_element_type=jnp.float32)
    term_y = lax.optimization_barrier(jnp.sum(weight_y.astype(jnp.float32), axis=1))[:, None] * y_block.astype(jnp.float32) - jnp.dot(weight_y, col_y, preferred_element_type=jnp.float32)
    return jnp.concatenate([term_x, term_y], axis=1)

def reference(x_embed, y_embed):
    factor = math.sqrt(D) / ANCHORS
    norm_x = squares(x_embed)
    norm_y = squares(y_embed)
    block_rows = math.gcd(ANCHORS, 512)

    def one_block(block_index):
        offset = (block_index * block_rows).astype(jnp.int32)
        x_block = lax.dynamic_slice_in_dim(x_embed, offset, block_rows, 0)
        y_block = lax.dynamic_slice_in_dim(y_embed, offset, block_rows, 0)
        return block_terms(x_block, y_block, x_embed, y_embed, norm_x, norm_y)
    stacked = lax.map(one_block, jnp.arange(ANCHORS // block_rows, dtype=jnp.int32))
    summed = stacked.reshape(ANCHORS, 2 * D)
    return (factor * summed[:, :D], -factor * summed[:, D:])
```

```python
import functools
import math

import jax
import jax.numpy as jnp
from jax import lax
from jax.experimental import pallas as pl
from jax.experimental.pallas import tpu as pltpu
from jax.sharding import PartitionSpec as P

MESH = pl.DeviceIdType.MESH
dist_eps = 0.0001

slot_offsets = ((0, 0, 0), (3, 0, 0), (1, 0, 0), (0, 3, 0), (1, 0, 1), (0, 1, 0), (0, 1, 3), (3, 1, 0), (0, 2, 0), (3, 2, 0), (1, 3, 0), (2, 0, 1), (2, 0, 2), (0, 1, 2), (0, 2, 2), (3, 2, 2), (1, 3, 3))
slot_total = 17
row_total = 7
row_parent = (-1, 0, 0, 0, 2, 0, 5)
row_gen = (-1, 1, 0, 3, 4, 2, 5)
slot_parent = ((-1, 0, 0, 0, 2, 0, 5, 5, 3, 7, 3, 4, 11, 6, 13, 14, 10), (-1, 0, 0, 0, 2, 0, 5, 5, 3, 7, 2, 4, 11, 6, 13, 14, 10))
slot_gen = ((-1, 1, 0, 3, 4, 2, 5, 1, 3, 2, 0, 0, 4, 5, 2, 1, 5), (-1, 1, 0, 3, 4, 2, 5, 1, 3, 2, 3, 0, 4, 5, 2, 1, 5))
kids = (((5, 2, 3, 1), (), (4,), (10, 8), (11,), (6, 7), (13,), (9,), (), (), (16,), (12,), (), (14,), (15,), (), ()), ((5, 2, 3, 1), (), (4, 10), (8,), (11,), (6, 7), (13,), (9,), (), (), (16,), (12,), (), (14,), (15,), (), ()))
pair_rows = (0, 0, 0, 6, 6, 4, 6, 6, 4, 4, 4, 5, 5, 3, 3, 3, 2, 2, 2, 2, 0, 0, 6, 4, 2, 1, 0, 0, 0, 6, 4, 4, 1, 1, 5, 6, 4, 5, 4, 1, 5, 3, 6, 1, 5, 2, 3, 3, 4, 4, 2, 2, 3, 0, 0, 3, 5, 0, 0, 0, 0, 0, 0, 0)
pair_cols = (0, 2, 5, 0, 4, 0, 7, 3, 6, 3, 7, 6, 4, 2, 6, 4, 6, 4, 3, 7, 6, 4, 1, 1, 1, 6, 3, 7, 1, 10, 10, 13, 10, 13, 10, 8, 8, 13, 14, 14, 11, 11, 12, 12, 12, 12, 14, 12, 9, 15, 9, 15, 15, 10, 13, 16, 16, 8, 11, 14, 12, 9, 15, 16)
first_use = {0: 0, 2: 1, 5: 2, 6: 3, 4: 4, 7: 6, 3: 7, 1: 22, 10: 29, 13: 31, 8: 35, 14: 38, 11: 40, 12: 42, 9: 48, 15: 49, 16: 55}
finish_at = {47: [6], 48: [1], 54: [4], 60: [3], 68: [2, 5]}
events = (
    {1: [(2, 0), (1, 0), (5, 0), (3, 0), (3, 1), (2, 1), (1, 1), (5, 1), (3, 2), (4, 0), (6, 0), (7, 0), (3, 3), (2, 2), (5, 2), (4, 1), (6, 1), (7, 1), (2, 3), (5, 3), (4, 2), (6, 2), (7, 2)], 3: [(10, 0), (9, 0), (4, 3), (6, 3), (11, 0), (7, 3)], 6: [(9, 1)], 7: [(13, 0)], 9: [(10, 1)], 10: [(12, 0)], 13: [(11, 1), (1, 2), (9, 2), (8, 0), (13, 1)], 16: [(14, 0)], 19: [(10, 2), (1, 3), (8, 1)], 20: [(12, 1), (13, 2)], 22: [(11, 2), (14, 1)], 25: [(15, 0), (8, 2)], 26: [(13, 3)], 29: [(10, 3), (14, 2), (12, 2)], 32: [(11, 3), (15, 1), (8, 3)], 35: [(14, 3)], 36: [(16, 0)], 38: [(15, 2)], 39: [(12, 3)], 42: [(16, 1)], 45: [(15, 3), (9, 3)], 48: [(16, 2)], 55: [(16, 3)]},
    {1: [(2, 0), (1, 0), (5, 0), (2, 1), (5, 1), (4, 0), (6, 0), (7, 0), (3, 0), (2, 2), (5, 2), (10, 0), (4, 1), (6, 1), (7, 1), (3, 1), (2, 3), (5, 3), (10, 1)], 2: [(4, 2), (6, 2)], 3: [(7, 2), (3, 2), (9, 0), (10, 2), (4, 3), (6, 3)], 6: [(11, 0), (7, 3), (3, 3)], 9: [(1, 1), (9, 1), (10, 3)], 10: [(13, 0)], 13: [(12, 0)], 16: [(11, 1), (1, 2), (8, 0), (13, 1)], 19: [(14, 0)], 22: [(1, 3), (8, 1)], 23: [(12, 1), (13, 2)], 25: [(11, 2), (14, 1)], 29: [(15, 0), (8, 2), (13, 3)], 32: [(14, 2), (12, 2), (16, 0)], 35: [(11, 3), (15, 1), (8, 3)], 38: [(14, 3)], 39: [(16, 1)], 41: [(15, 2), (9, 2)], 42: [(12, 3)], 45: [(16, 2)], 48: [(15, 3), (9, 3)], 52: [(16, 3)]},
)

step_total = len(pair_rows)
lag = 4
ring = 8
pieces = 4
moves = ((1, 0, 0), (3, 0, 0), (0, 1, 0), (0, 3, 0), (0, 0, 1), (0, 0, 3))


def packed(values, bits):
    per = 30 // bits
    words = []
    for first in range(0, len(values), per):
        word = 0
        for place, value in enumerate(values[first : first + per]):
            word |= value << (bits * place)
        words.append(word)
    return per, bits, words


def lookup(table, k):
    per, bits, words = table
    which = k // per
    word = jnp.int32(words[0])
    for index in range(1, len(words)):
        word = jnp.where(which >= index, jnp.int32(words[index]), word)
    return (word >> ((k - which * per) * bits)) & ((1 << bits) - 1)


def norm_plan():
    lists = {}
    for slot, k in sorted(first_use.items(), key=lambda item: item[1]):
        lists.setdefault(k, []).append(slot)
    return lists


def kernel(x_ref, y_ref, gx_ref, gy_ref, held, total, weight_sum, norm_col, norm_row, stage, rho, own_d, other_d,
           out_part, in_part, out_sum, in_sum, mean_row, sum_col, land,
           got_sem, sent_sem, half_sem, d_sent, d_got, part_sent, part_got, sum_sent, sum_got, land_sem):
    half, width = x_ref.shape
    block = 2 * half
    piece = block // pieces
    gx, gy = lax.axis_index("gx"), lax.axis_index("gy")
    px, pz_hi = gx // 2, gx % 2
    py, pz_lo, core = gy // 4, (gy // 2) % 2, gy % 2
    pz = pz_hi * 2 + pz_lo
    factor = math.sqrt(width) / (block * 64)

    def place(move):
        cx, cy, cz = (px + move[0]) % 4, (py + move[1]) % 4, (pz + move[2]) % 4
        return (cx * 2 + cz // 2, (cy * 2 + cz % 2) * 2 + core)

    near = [place(move) for move in moves]
    partner = (gx, gy + 1 - 2 * core)

    def piece_rows(q):
        side = core if q < pieces // 2 else 1 - core
        return pl.ds(pl.multiple_of(side * half + (q % (pieces // 2)) * piece, piece), piece)

    def block_copy(parent, child, q, gen):
        return pltpu.make_async_remote_copy(
            src_ref=held.at[parent, piece_rows(q)],
            dst_ref=held.at[child, piece_rows(q)],
            send_sem=sent_sem.at[child, q],
            recv_sem=got_sem.at[child, q],
            device_id=near[gen ^ 1],
            device_id_type=MESH,
        )

    def half_copy():
        rows = pl.ds(pl.multiple_of(core * half, half), half)
        return pltpu.make_async_remote_copy(
            src_ref=stage, dst_ref=held.at[0, rows], send_sem=half_sem.at[0], recv_sem=half_sem.at[1],
            device_id=partner, device_id_type=MESH,
        )

    def d_copy(slot):
        return pltpu.make_async_remote_copy(
            src_ref=own_d.at[slot], dst_ref=other_d.at[slot], send_sem=d_sent.at[slot], recv_sem=d_got.at[slot],
            device_id=partner, device_id_type=MESH,
        )

    def part_copy(r, q):
        rows = pl.ds(q * piece, piece)
        return pltpu.make_async_remote_copy(
            src_ref=out_part.at[r - 1, rows], dst_ref=in_part.at[r - 1, rows],
            send_sem=part_sent.at[r - 1, q], recv_sem=part_got.at[r - 1, q],
            device_id=near[row_gen[r]], device_id_type=MESH,
        )

    def sum_copy(r):
        return pltpu.make_async_remote_copy(
            src_ref=out_sum.at[r - 1], dst_ref=in_sum.at[r - 1],
            send_sem=sum_sent.at[r - 1], recv_sem=sum_got.at[r - 1],
            device_id=near[row_gen[r]], device_id_type=MESH,
        )

    first = core == 0
    own_rows = pl.ds(pl.multiple_of(core * half, half), half)
    held[0, own_rows] = jnp.where(first, x_ref[...], y_ref[...])
    stage[...] = jnp.where(first, y_ref[...], x_ref[...])

    barrier = pltpu.get_barrier_semaphore()
    for other in [partner] + near:
        pl.semaphore_signal(barrier, inc=1, device_id=other, device_id_type=MESH)
    pl.semaphore_wait(barrier, 7)

    half_copy().start()

    def send_on(c, slot, q):
        for child in kids[c][slot]:
            block_copy(slot, child, q, slot_gen[c][child]).start()

    def event(c, slot, q):
        parent = slot_parent[c][slot]
        block_copy(parent, slot, q, slot_gen[c][slot]).wait_recv()
        send_on(c, slot, q)

    def on_core(c, events):
        @pl.when(core == c)
        def _():
            for slot, q in events:
                event(c, slot, q)

    for c in (0, 1):

        @pl.when(core == c)
        def _(c=c):
            for q in range(pieces // 2):
                send_on(c, 0, q)

    half_copy().wait()

    for c in (0, 1):

        @pl.when(core == c)
        def _(c=c):
            for q in range(pieces // 2, pieces):
                send_on(c, 0, q)

    def clear(index, _):
        r = index // pieces
        rows = pl.ds(pl.multiple_of((index % pieces) * piece, piece), piece)
        total[r, rows] = jnp.zeros((piece, width), jnp.float32)
        weight_sum[r, rows] = jnp.zeros((piece, 128), jnp.float32)
        return 0

    lax.fori_loop(0, row_total * pieces, clear, 0)

    def norms(slot):
        def part(q, _):
            rows = pl.ds(pl.multiple_of(q * piece, piece), piece)
            wide = held[slot, rows].astype(jnp.float32)
            sums = jnp.sum(wide * wide, axis=1, keepdims=True)
            norm_col[slot, rows] = jnp.broadcast_to(sums, (piece, 128))
            return 0

        lax.fori_loop(0, pieces, part, 0)
        norm_row[slot] = jnp.transpose(norm_col[slot])[0:8, :] + dist_eps

    pair_r = packed(pair_rows, 3)
    pair_t = packed(pair_cols, 5)
    norm_at = norm_plan()

    def before(k, low, high):
        for step in range(low, high):
            for c in (0, 1):
                if step in events[c]:

                    @pl.when(jnp.logical_and(k == step, core == c))
                    def _(c=c, step=step):
                        for slot, q in events[c][step]:
                            event(c, slot, q)

            for slot in norm_at.get(step, ()):

                @pl.when(k == step)
                def _(slot=slot):
                    norms(slot)

            for r in finish_at.get(step, ()):

                @pl.when(k == step)
                def _(r=r):
                    finish(r)

    def stage_a(k):
        r, t = lookup(pair_r, k), lookup(pair_t, k)
        slot = k % ring
        gram = lax.dot_general(held[r], held[t], (((1,), (1,)), ((), ())), preferred_element_type=jnp.float32)
        left = norm_col[r]
        square = (jnp.concatenate([left] * (block // 128), axis=1) + norm_row[t][0:1, :]) - 2.0 * gram
        square = jnp.maximum(square, 1e-20)
        inverse = lax.rsqrt(square)
        rho[slot] = inverse
        own_d[slot] = square * inverse

    def stage_b(k):
        r, t = lookup(pair_r, k), lookup(pair_t, k)
        slot = k % ring
        weight = (1.0 - other_d[slot] * rho[slot]).astype(jnp.bfloat16)
        total[r] += jnp.dot(weight, held[t], preferred_element_type=jnp.float32)
        wide = weight.astype(jnp.float32)
        part = wide[:, 0:128]
        for first_col in range(128, block, 128):
            part = part + wide[:, first_col : first_col + 128]
        weight_sum[r] += part

    def column_mean(r):
        mean = jnp.sum(held[r].astype(jnp.float32), axis=0, keepdims=True) * (1.0 / block)
        mean_row[...] = jnp.broadcast_to(mean, (8, width))

    def row_sums(r):
        sums = jnp.sum(weight_sum[r], axis=1, keepdims=True)
        sum_col[...] = jnp.broadcast_to(sums, (block, 128))

    def kids_of(r):
        return [s for s in range(row_total) if row_parent[s] == r]

    strip = 16

    def finish(r):
        column_mean(r)
        row_sums(r)
        sums = jnp.transpose(sum_col[...])[0:8, :]
        for s in kids_of(r):
            sum_copy(s).wait_recv()
            sums = sums + in_sum[s - 1]
        out_sum[r - 1] = sums
        sum_copy(r).start()
        for q in range(pieces):
            for s in kids_of(r):
                part_copy(s, q).wait_recv()

            def some(i, _, q=q):
                rows = pl.ds(pl.multiple_of(q * piece + i * strip, strip), strip)
                scale = jnp.concatenate([sum_col[rows]] * (width // 128), axis=1)
                value = total[r, rows] - scale * mean_row[0:1, :]
                for s in kids_of(r):
                    value = value + in_part[s - 1, rows].astype(jnp.float32)
                out_part[r - 1, rows] = value.astype(jnp.bfloat16)
                return 0

            lax.fori_loop(0, piece // strip, some, 0)
            part_copy(r, q).start()

    def iteration_a(k, _):
        before(k, 0, lag)
        stage_a(k)
        d_copy(k % ring).start()
        return 0

    def iteration_ab(k, _):
        before(k, lag, step_total)
        d_copy((k - lag) % ring).wait_recv()

        @pl.when(k >= ring)
        def _():
            d_copy(k % ring).wait_send()

        stage_a(k)
        stage_b(k - lag)
        d_copy(k % ring).start()
        return 0

    def iteration_b(k, _):
        before(k, step_total, step_total + lag)
        d_copy((k - lag) % ring).wait_recv()
        stage_b(k - lag)
        return 0

    lax.fori_loop(0, lag, iteration_a, 0)
    lax.fori_loop(lag, step_total, iteration_ab, 0)
    lax.fori_loop(step_total, step_total + lag, iteration_b, 0)
    for r in finish_at.get(step_total + lag, ()):
        finish(r)

    column_mean(0)
    row_sums(0)
    sums = jnp.transpose(sum_col[...])[0:8, :]
    for s in kids_of(0):
        sum_copy(s).wait_recv()
        sums = sums + in_sum[s - 1]
    whole = jnp.transpose(jnp.concatenate([sums] * 16, axis=0))
    norm_col[0] = whole

    def result(q, target):
        for s in kids_of(0):
            part_copy(s, q).wait_recv()

    for q in range(pieces):
        for s in kids_of(0):
            part_copy(s, q).wait_recv()

    def final_rows(i, target, side):
        rows = pl.ds(pl.multiple_of(side * half + i * strip, strip), strip)
        here = pl.ds(pl.multiple_of(i * strip, strip), strip)
        own_scale = jnp.concatenate([sum_col[rows]] * (width // 128), axis=1)
        scale = jnp.concatenate([norm_col[0, rows]] * (width // 128), axis=1)
        mean = mean_row[0:1, :]
        value = total[0, rows] - own_scale * mean
        for s in kids_of(0):
            value = value + in_part[s - 1, rows].astype(jnp.float32)
        target[here] = factor * (scale * (held[0, rows].astype(jnp.float32) - mean) - value)

    def land_copy():
        return pltpu.make_async_remote_copy(
            src_ref=land.at[0], dst_ref=land.at[1], send_sem=land_sem.at[0], recv_sem=land_sem.at[1],
            device_id=partner, device_id_type=MESH,
        )

    def theirs(i, _):
        final_rows(i, land.at[0], 1 - core)
        return 0

    def ours(i, _):
        final_rows(i, land.at[2], core)
        return 0

    lax.fori_loop(0, half // strip, theirs, 0)
    land_copy().start()
    lax.fori_loop(0, half // strip, ours, 0)

    for c in (0, 1):

        @pl.when(core == c)
        def _(c=c):
            for child in range(1, slot_total):
                for q in range(pieces):
                    block_copy(slot_parent[c][child], child, q, slot_gen[c][child]).wait_send()

    for r in range(1, row_total):
        sum_copy(r).wait_send()
        for q in range(pieces):
            part_copy(r, q).wait_send()
    for slot in range(ring):
        d_copy(slot).wait_send()
    land_copy().wait()
    gx_ref[...] = jnp.where(first, land[2], land[1])
    gy_ref[...] = jnp.where(first, land[1], land[2])


def per_device(x_embed, y_embed):
    half, width = x_embed.shape
    block = 2 * half
    out = jax.ShapeDtypeStruct((half, width), jnp.float32)
    dma = pltpu.SemaphoreType.DMA
    return pl.pallas_call(
        kernel,
        out_shape=(out, out),
        in_specs=[pl.BlockSpec(memory_space=pltpu.VMEM)] * 2,
        out_specs=[pl.BlockSpec(memory_space=pltpu.VMEM)] * 2,
        scratch_shapes=[
            pltpu.VMEM((slot_total, block, width), jnp.bfloat16),
            pltpu.VMEM((row_total, block, width), jnp.float32),
            pltpu.VMEM((row_total, block, 128), jnp.float32),
            pltpu.VMEM((slot_total, block, 128), jnp.float32),
            pltpu.VMEM((slot_total, 8, block), jnp.float32),
            pltpu.VMEM((half, width), jnp.bfloat16),
            pltpu.VMEM((ring, block, block), jnp.float32),
            pltpu.VMEM((ring, block, block), jnp.float32),
            pltpu.VMEM((ring, block, block), jnp.float32),
            pltpu.VMEM((row_total - 1, block, width), jnp.bfloat16),
            pltpu.VMEM((row_total - 1, block, width), jnp.bfloat16),
            pltpu.VMEM((row_total - 1, 8, block), jnp.float32),
            pltpu.VMEM((row_total - 1, 8, block), jnp.float32),
            pltpu.VMEM((8, width), jnp.float32),
            pltpu.VMEM((block, 128), jnp.float32),
            pltpu.VMEM((3, half, width), jnp.float32),
            dma((slot_total, pieces)),
            dma((slot_total, pieces)),
            dma((2,)),
            dma((ring,)),
            dma((ring,)),
            dma((row_total - 1, pieces)),
            dma((row_total - 1, pieces)),
            dma((row_total - 1,)),
            dma((row_total - 1,)),
            dma((2,)),
        ],
        compiler_params=pltpu.CompilerParams(
            collective_id=0, has_side_effects=True, vmem_limit_bytes=56 * 2**20
        ),
        cost_estimate=pl.CostEstimate(
            flops=4 * step_total * block * block * width,
            bytes_accessed=12 * half * width,
            transcendentals=step_total * block * block,
        ),
        name="relational",
    )(x_embed, y_embed)


def solution(mesh):
    spec = P(("gx", "gy"), None)
    return jax.shard_map(
        per_device, mesh=mesh, in_specs=(spec, spec), out_specs=(spec, spec), check_vma=False
    )
```

```python
import functools
import math

import jax
import jax.numpy as jnp
from jax import lax
from jax.experimental import pallas as pl
from jax.experimental.pallas import tpu as pltpu
from jax.sharding import PartitionSpec as P

MESH = pl.DeviceIdType.MESH
dist_eps = 0.0001

slot_offsets = ((0, 0, 0), (3, 0, 0), (1, 0, 0), (0, 3, 0), (1, 0, 1), (0, 1, 0), (0, 1, 3), (3, 1, 0), (0, 2, 0), (3, 2, 0), (1, 3, 0), (2, 0, 1), (2, 0, 2), (0, 1, 2), (0, 2, 2), (3, 2, 2), (1, 3, 3))
slot_total = 17
row_total = 7
row_parent = (-1, 0, 0, 0, 2, 0, 5)
row_gen = (-1, 1, 0, 3, 4, 2, 5)
slot_parent = ((-1, 0, 0, 0, 2, 0, 5, 5, 3, 7, 3, 4, 11, 6, 13, 14, 10), (-1, 0, 0, 0, 2, 0, 5, 5, 3, 7, 2, 4, 11, 6, 13, 14, 10))
slot_gen = ((-1, 1, 0, 3, 4, 2, 5, 1, 3, 2, 0, 0, 4, 5, 2, 1, 5), (-1, 1, 0, 3, 4, 2, 5, 1, 3, 2, 3, 0, 4, 5, 2, 1, 5))
kids = (((5, 2, 3, 1), (), (4,), (10, 8), (11,), (6, 7), (13,), (9,), (), (), (16,), (12,), (), (14,), (15,), (), ()), ((5, 2, 3, 1), (), (4, 10), (8,), (11,), (6, 7), (13,), (9,), (), (), (16,), (12,), (), (14,), (15,), (), ()))
groups = (((0, 0),), ((0, 2), (0, 5)), ((6, 0), (6, 4), (4, 0)), ((4, 6), (5, 6), (5, 4)), ((6, 7), (6, 3), (4, 3)), ((4, 7), (3, 2), (3, 6)), ((3, 4), (2, 6), (2, 4)), ((2, 3), (2, 7), (0, 6)), ((0, 4), (0, 3), (0, 7)), ((6, 1), (4, 1), (2, 1)), ((1, 6), (0, 1)), ((6, 10), (4, 10), (1, 10)), ((4, 13), (1, 13), (5, 10)), ((5, 13), (0, 10), (0, 13)), ((6, 8), (4, 8), (5, 11)), ((4, 14), (1, 14), (3, 11)), ((3, 14), (0, 8), (0, 11)), ((6, 12), (1, 12), (5, 12)), ((2, 12), (3, 12), (0, 14)), ((4, 9), (4, 15), (2, 9)), ((2, 15), (3, 15), (0, 12)), ((0, 9), (0, 15)), ((3, 16), (5, 16), (0, 16)))
first_use = {0: 0, 2: 1, 5: 1, 6: 2, 4: 2, 7: 4, 3: 4, 1: 9, 10: 11, 13: 12, 8: 14, 11: 14, 14: 15, 12: 17, 9: 19, 15: 19, 16: 22}
finish_at = {21: [1, 6], 23: [4], 26: [3, 5, 2]}
events = (
    {1: [(2, 0), (1, 0), (5, 0), (3, 0), (3, 1), (2, 1), (1, 1), (5, 1), (3, 2), (4, 0), (6, 0), (7, 0), (3, 3), (2, 2), (5, 2), (4, 1), (6, 1), (7, 1), (2, 3), (5, 3), (4, 2), (6, 2), (7, 2)], 2: [(10, 0), (9, 0), (4, 3), (6, 3), (11, 0), (7, 3)], 4: [(9, 1), (13, 0)], 5: [(10, 1), (12, 0)], 6: [(11, 1), (1, 2), (9, 2), (8, 0)], 7: [(13, 1), (14, 0)], 8: [(10, 2), (1, 3), (8, 1)], 9: [(12, 1), (13, 2), (11, 2), (14, 1)], 11: [(15, 0), (8, 2), (13, 3), (10, 3), (14, 2)], 12: [(12, 2)], 13: [(11, 3), (15, 1), (8, 3)], 14: [(14, 3)], 15: [(16, 0), (15, 2)], 16: [(12, 3)], 17: [(16, 1)], 18: [(15, 3), (9, 3)], 19: [(16, 2)], 22: [(16, 3)]},
    {1: [(2, 0), (1, 0), (5, 0), (2, 1), (5, 1), (4, 0), (6, 0), (7, 0), (3, 0), (2, 2), (5, 2), (10, 0), (4, 1), (6, 1), (7, 1), (3, 1), (2, 3), (5, 3), (10, 1)], 2: [(4, 2), (6, 2), (7, 2), (3, 2), (9, 0), (10, 2), (4, 3), (6, 3)], 4: [(11, 0), (7, 3), (3, 3)], 5: [(1, 1), (9, 1), (10, 3), (13, 0)], 7: [(12, 0), (11, 1), (1, 2), (8, 0)], 8: [(13, 1), (14, 0)], 9: [(1, 3), (8, 1)], 10: [(12, 1), (13, 2)], 11: [(11, 2), (14, 1), (15, 0), (8, 2)], 12: [(13, 3)], 13: [(14, 2), (12, 2), (16, 0)], 14: [(11, 3), (15, 1), (8, 3)], 15: [(14, 3)], 16: [(16, 1), (15, 2), (9, 2)], 17: [(12, 3)], 18: [(16, 2)], 19: [(15, 3), (9, 3)], 21: [(16, 3)]},
)
lag = 3
ring = 18

group_total = len(groups)
pieces = 4
moves = ((1, 0, 0), (3, 0, 0), (0, 1, 0), (0, 3, 0), (0, 0, 1), (0, 0, 3))
numbers = []
for group in groups:
    numbers.append(tuple(range(sum(map(len, numbers)), sum(map(len, numbers)) + len(group))))
first_group = {}
for index, group in enumerate(groups):
    for r, _ in group:
        first_group.setdefault(r, index)
step_total = sum(map(len, groups))


def kernel(x_ref, y_ref, gx_ref, gy_ref, held, total, weight_sum, norm_col, norm_row, stage, rho, own_d, other_d,
           out_part, in_part, out_sum, in_sum, mean_row, sum_col, land,
           got_sem, sent_sem, half_sem, d_sent, d_got, part_sent, part_got, sum_sent, sum_got, land_sem):
    half, width = x_ref.shape
    block = 2 * half
    piece = block // pieces
    gx, gy = lax.axis_index("gx"), lax.axis_index("gy")
    px, pz_hi = gx // 2, gx % 2
    py, pz_lo, core = gy // 4, (gy // 2) % 2, gy % 2
    pz = pz_hi * 2 + pz_lo
    factor = math.sqrt(width) / (block * 64)

    def place(move):
        cx, cy, cz = (px + move[0]) % 4, (py + move[1]) % 4, (pz + move[2]) % 4
        return (cx * 2 + cz // 2, (cy * 2 + cz % 2) * 2 + core)

    near = [place(move) for move in moves]
    partner = (gx, gy + 1 - 2 * core)

    def piece_rows(q):
        side = core if q < pieces // 2 else 1 - core
        return pl.ds(pl.multiple_of(side * half + (q % (pieces // 2)) * piece, piece), piece)

    def block_copy(parent, child, q, gen):
        return pltpu.make_async_remote_copy(
            src_ref=held.at[parent, piece_rows(q)],
            dst_ref=held.at[child, piece_rows(q)],
            send_sem=sent_sem.at[child, q],
            recv_sem=got_sem.at[child, q],
            device_id=near[gen ^ 1],
            device_id_type=MESH,
        )

    def half_copy():
        rows = pl.ds(pl.multiple_of(core * half, half), half)
        return pltpu.make_async_remote_copy(
            src_ref=stage, dst_ref=held.at[0, rows], send_sem=half_sem.at[0], recv_sem=half_sem.at[1],
            device_id=partner, device_id_type=MESH,
        )

    def d_copy(slot):
        return pltpu.make_async_remote_copy(
            src_ref=own_d.at[slot], dst_ref=other_d.at[slot], send_sem=d_sent.at[slot], recv_sem=d_got.at[slot],
            device_id=partner, device_id_type=MESH,
        )

    def part_copy(r, q):
        rows = pl.ds(q * piece, piece)
        return pltpu.make_async_remote_copy(
            src_ref=out_part.at[r - 1, rows], dst_ref=in_part.at[r - 1, rows],
            send_sem=part_sent.at[r - 1, q], recv_sem=part_got.at[r - 1, q],
            device_id=near[row_gen[r]], device_id_type=MESH,
        )

    def sum_copy(r):
        return pltpu.make_async_remote_copy(
            src_ref=out_sum.at[r - 1], dst_ref=in_sum.at[r - 1],
            send_sem=sum_sent.at[r - 1], recv_sem=sum_got.at[r - 1],
            device_id=near[row_gen[r]], device_id_type=MESH,
        )

    first = core == 0
    own_rows = pl.ds(pl.multiple_of(core * half, half), half)
    held[0, own_rows] = jnp.where(first, x_ref[...], y_ref[...])
    stage[...] = jnp.where(first, y_ref[...], x_ref[...])

    barrier = pltpu.get_barrier_semaphore()
    for other in [partner] + near:
        pl.semaphore_signal(barrier, inc=1, device_id=other, device_id_type=MESH)
    pl.semaphore_wait(barrier, 7)

    half_copy().start()

    def send_on(c, slot, q):
        for child in kids[c][slot]:
            block_copy(slot, child, q, slot_gen[c][child]).start()

    def event(c, slot, q):
        parent = slot_parent[c][slot]
        block_copy(parent, slot, q, slot_gen[c][slot]).wait_recv()
        send_on(c, slot, q)

    def on_core(c, events):
        @pl.when(core == c)
        def _():
            for slot, q in events:
                event(c, slot, q)

    for c in (0, 1):

        @pl.when(core == c)
        def _(c=c):
            for q in range(pieces // 2):
                send_on(c, 0, q)

    half_copy().wait()

    for c in (0, 1):

        @pl.when(core == c)
        def _(c=c):
            for q in range(pieces // 2, pieces):
                send_on(c, 0, q)

    def norms(slot):
        wide = held[slot].astype(jnp.float32)
        square = wide * wide
        part = square[:, 0:128]
        for col in range(128, width, 128):
            part = part + square[:, col : col + 128]
        turned = jnp.sum(jnp.transpose(part), axis=0, keepdims=True) + dist_eps
        norm_row[slot] = jnp.broadcast_to(turned, (8, block))
        if slot < row_total:
            norm_col[slot] = jnp.broadcast_to(jnp.sum(part, axis=1, keepdims=True), (block, 128))
            mean = jnp.sum(wide, axis=0, keepdims=True) * (1.0 / block)
            mean_row[slot] = jnp.broadcast_to(mean, (8, width))

    def stage_a(k, r, t):
        slot = k % ring
        gram = lax.dot_general(held[r], held[t], (((1,), (1,)), ((), ())), preferred_element_type=jnp.float32)
        left = jnp.concatenate([norm_col[r]] * (block // 128), axis=1)
        square = (left + norm_row[t][0:1, :]) - 2.0 * gram
        square = jnp.maximum(square, 1e-20)
        inverse = lax.rsqrt(square)
        rho[slot] = inverse
        own_d[slot] = square * inverse

    def stage_b(index):
        rows_here = sorted({r for r, _ in groups[index]})
        for r in rows_here:
            new = first_group[r] == index
            value = None if new else total[r]
            sums = None if new else weight_sum[r]
            for k, (row, t) in zip(numbers[index], groups[index]):
                if row != r:
                    continue
                slot = k % ring
                weight = (1.0 - other_d[slot] * rho[slot]).astype(jnp.bfloat16)
                term = jnp.dot(weight, held[t], preferred_element_type=jnp.float32)
                value = term if value is None else value + term
                wide = weight.astype(jnp.float32)
                for col in range(0, block, 128):
                    part = wide[:, col : col + 128]
                    sums = part if sums is None else sums + part
            total[r] = value
            weight_sum[r] = sums

    def row_sums(r):
        sums = jnp.sum(weight_sum[r], axis=1, keepdims=True)
        sum_col[r] = jnp.broadcast_to(sums, (block, 128))

    def kids_of(r):
        return [s for s in range(row_total) if row_parent[s] == r]

    def finish_wait(r):
        for s in kids_of(r):
            sum_copy(s).wait_recv()
            for q in range(pieces):
                part_copy(s, q).wait_recv()

    def finish_compute(r):
        row_sums(r)
        sums = jnp.transpose(sum_col[r])[0:8, :]
        for s in kids_of(r):
            sums = sums + in_sum[s - 1]
        out_sum[r - 1] = sums
        for q in range(pieces):
            rows = pl.ds(q * piece, piece)
            scale = jnp.concatenate([sum_col[r, rows]] * (width // 128), axis=1)
            value = total[r, rows] - scale * mean_row[r, 0:1, :]
            for s in kids_of(r):
                value = value + in_part[s - 1, rows].astype(jnp.float32)
            out_part[r - 1, rows] = value.astype(jnp.bfloat16)

    def finish_send(r):
        sum_copy(r).start()
        for q in range(pieces):
            part_copy(r, q).start()

    for index in range(group_total + lag):
        for c in (0, 1):
            if index in events[c]:
                on_core(c, events[c][index])
        back = index - lag
        done = finish_at.get(index, ())
        for r in done:
            finish_wait(r)
        if back >= 0:
            for k in numbers[back]:
                d_copy(k % ring).wait_recv()
        if index < group_total:
            for k in numbers[index]:
                if k >= ring:
                    d_copy(k % ring).wait_send()
        for slot in sorted(first_use):
            if first_use[slot] == index:
                norms(slot)
        if index < group_total:
            for k, (r, t) in zip(numbers[index], groups[index]):
                stage_a(k, r, t)
        if back >= 0:
            stage_b(back)
        for r in done:
            finish_compute(r)
        if index < group_total:
            for k in numbers[index]:
                d_copy(k % ring).start()
        for r in done:
            finish_send(r)
    for r in finish_at.get(group_total + lag, ()):
        finish_wait(r)
        finish_compute(r)
        finish_send(r)

    row_sums(0)
    sums = jnp.transpose(sum_col[0])[0:8, :]
    for s in kids_of(0):
        sum_copy(s).wait_recv()
        sums = sums + in_sum[s - 1]
    norm_col[0] = jnp.transpose(jnp.concatenate([sums] * 16, axis=0))
    for s in kids_of(0):
        for q in range(pieces):
            part_copy(s, q).wait_recv()

    def final_rows(place_to, side):
        for i in range(half // piece):
            rows = pl.ds(pl.multiple_of(side * half + i * piece, piece), piece)
            own_scale = jnp.concatenate([sum_col[0, rows]] * (width // 128), axis=1)
            scale = jnp.concatenate([norm_col[0, rows]] * (width // 128), axis=1)
            mean = mean_row[0, 0:1, :]
            value = total[0, rows] - own_scale * mean
            for s in kids_of(0):
                value = value + in_part[s - 1, rows].astype(jnp.float32)
            here = pl.ds(i * piece, piece)
            land[place_to, here] = factor * (scale * (held[0, rows].astype(jnp.float32) - mean) - value)

    def land_copy():
        return pltpu.make_async_remote_copy(
            src_ref=land.at[0], dst_ref=land.at[1], send_sem=land_sem.at[0], recv_sem=land_sem.at[1],
            device_id=partner, device_id_type=MESH,
        )

    final_rows(0, 1 - core)
    land_copy().start()
    final_rows(2, core)

    for c in (0, 1):

        @pl.when(core == c)
        def _(c=c):
            for child in range(1, slot_total):
                for q in range(pieces):
                    block_copy(slot_parent[c][child], child, q, slot_gen[c][child]).wait_send()

    for r in range(1, row_total):
        sum_copy(r).wait_send()
        for q in range(pieces):
            part_copy(r, q).wait_send()
    for slot in range(ring):
        d_copy(slot).wait_send()
    land_copy().wait()
    gx_ref[...] = jnp.where(first, land[2], land[1])
    gy_ref[...] = jnp.where(first, land[1], land[2])


def per_device(x_embed, y_embed):
    half, width = x_embed.shape
    block = 2 * half
    out = jax.ShapeDtypeStruct((half, width), jnp.float32)
    dma = pltpu.SemaphoreType.DMA
    return pl.pallas_call(
        kernel,
        out_shape=(out, out),
        in_specs=[pl.BlockSpec(memory_space=pltpu.VMEM)] * 2,
        out_specs=[pl.BlockSpec(memory_space=pltpu.VMEM)] * 2,
        scratch_shapes=[
            pltpu.VMEM((slot_total, block, width), jnp.bfloat16),
            pltpu.VMEM((row_total, block, width), jnp.float32),
            pltpu.VMEM((row_total, block, 128), jnp.float32),
            pltpu.VMEM((row_total, block, 128), jnp.float32),
            pltpu.VMEM((slot_total, 8, block), jnp.float32),
            pltpu.VMEM((half, width), jnp.bfloat16),
            pltpu.VMEM((ring, block, block), jnp.float32),
            pltpu.VMEM((ring, block, block), jnp.float32),
            pltpu.VMEM((ring, block, block), jnp.float32),
            pltpu.VMEM((row_total - 1, block, width), jnp.bfloat16),
            pltpu.VMEM((row_total - 1, block, width), jnp.bfloat16),
            pltpu.VMEM((row_total - 1, 8, block), jnp.float32),
            pltpu.VMEM((row_total - 1, 8, block), jnp.float32),
            pltpu.VMEM((row_total, 8, width), jnp.float32),
            pltpu.VMEM((row_total, block, 128), jnp.float32),
            pltpu.VMEM((3, half, width), jnp.float32),
            dma((slot_total, pieces)),
            dma((slot_total, pieces)),
            dma((2,)),
            dma((ring,)),
            dma((ring,)),
            dma((row_total - 1, pieces)),
            dma((row_total - 1, pieces)),
            dma((row_total - 1,)),
            dma((row_total - 1,)),
            dma((2,)),
        ],
        compiler_params=pltpu.CompilerParams(
            collective_id=0, has_side_effects=True, vmem_limit_bytes=56 * 2**20
        ),
        cost_estimate=pl.CostEstimate(
            flops=4 * step_total * block * block * width,
            bytes_accessed=12 * half * width,
            transcendentals=step_total * block * block,
        ),
        name="relational",
    )(x_embed, y_embed)


def solution(mesh):
    spec = P(("gx", "gy"), None)
    return jax.shard_map(
        per_device, mesh=mesh, in_specs=(spec, spec), out_specs=(spec, spec), check_vma=False
    )
```

```python
import functools
import math

import jax
import jax.numpy as jnp
from jax import lax
from jax.experimental import pallas as pl
from jax.experimental.pallas import tpu as pltpu
from jax.sharding import PartitionSpec as P

MESH = pl.DeviceIdType.MESH
dist_eps = 0.0001

slot_offsets = ((0, 0, 0), (0, 1, 0), (3, 0, 0), (0, 0, 1), (1, 0, 0), (0, 0, 3), (0, 3, 0), (2, 0, 0), (0, 2, 0), (3, 2, 0), (2, 0, 1), (3, 2, 1), (0, 0, 2), (0, 1, 2), (1, 1, 2), (1, 2, 2), (0, 3, 2), (1, 3, 2), (2, 2, 3), (3, 2, 3))
slot_total = 20
row_total = 7
row_parent = (-1, 0, 0, 0, 0, 0, 0)
row_gen = (-1, 2, 1, 4, 0, 5, 3)
slot_parent = ((-1, 0, 0, 0, 0, 0, 0, 2, 6, 8, 7, 9, 3, 12, 13, 14, 12, 16, 19, 9), (-1, 0, 0, 0, 0, 0, 0, 4, 6, 8, 7, 9, 5, 12, 13, 14, 12, 16, 19, 9))
slot_gen = ((-1, 2, 1, 4, 0, 5, 3, 1, 3, 1, 4, 4, 4, 2, 0, 2, 3, 0, 1, 5), (-1, 2, 1, 4, 0, 5, 3, 0, 3, 1, 4, 4, 5, 2, 0, 2, 3, 0, 1, 5))
kids = (((6, 3, 2, 4, 1, 5), (), (7,), (12,), (), (), (8,), (10,), (9,), (19, 11), (), (), (13, 16), (14,), (15,), (), (17,), (), (), (18,)), ((6, 5, 4, 2, 1, 3), (), (), (), (7,), (12,), (8,), (10,), (9,), (19, 11), (), (), (13, 16), (14,), (15,), (), (17,), (), (), (18,)))
groups = (((0, 0),), ((0, 6), (0, 1)), ((1, 7), (6, 7)), ((0, 7), (0, 12)), ((4, 12), (1, 2)), ((4, 5), (1, 5)), ((6, 2), (6, 5)), ((2, 6), (2, 1)), ((2, 12), (2, 5)), ((5, 6), (5, 1)), ((5, 2), (5, 4)), ((0, 2), (0, 4)), ((2, 8), (5, 8)), ((0, 5), (0, 8)), ((4, 13), (6, 13)), ((0, 13),), ((4, 9), (0, 9)), ((2, 14), (5, 14)), ((0, 14),), ((4, 16), (3, 7)), ((6, 19), (1, 19)), ((2, 15), (5, 15)), ((3, 8), (3, 14)), ((5, 10), (3, 19)), ((3, 15), (1, 10)), ((6, 10), (0, 16)), ((0, 3), (0, 19)), ((4, 11), (6, 11)), ((6, 18), (1, 11)), ((1, 18), (5, 17)), ((2, 17), (3, 17)), ((0, 15), (0, 10)), ((0, 11), (0, 18)), ((0, 17),))
first_use = {0: 0, 6: 1, 1: 1, 7: 2, 12: 3, 4: 4, 2: 4, 5: 5, 8: 12, 13: 14, 9: 16, 14: 17, 16: 19, 3: 19, 19: 20, 15: 21, 10: 23, 11: 27, 18: 28, 17: 29}
finish_at = {31: [4], 32: [6], 33: [1, 5], 34: [2, 3]}
events = (
    {1: [(2, 0), (1, 0), (6, 0), (3, 0), (2, 1), (3, 1), (2, 2), (1, 1), (6, 1), (3, 2), (2, 3), (3, 3), (4, 0), (1, 2), (6, 2), (5, 0), (7, 0), (12, 0), (7, 1), (1, 3), (6, 3), (12, 1), (7, 2), (12, 2)], 2: [(7, 3), (8, 0), (12, 3)], 4: [(4, 1), (5, 1), (13, 0), (4, 2), (8, 1), (5, 2), (4, 3), (10, 0), (5, 3)], 5: [(13, 1)], 6: [(8, 2), (9, 0)], 8: [(10, 1), (13, 2), (14, 0)], 10: [(8, 3), (9, 1)], 12: [(13, 3), (14, 1)], 13: [(16, 0), (10, 2)], 14: [(9, 2), (19, 0)], 15: [(11, 0), (14, 2), (15, 0)], 16: [(16, 1), (9, 3), (19, 1), (11, 1)], 17: [(14, 3), (15, 1), (16, 2), (19, 2)], 18: [(18, 0)], 19: [(11, 2), (17, 0), (15, 2), (16, 3), (19, 3), (18, 1)], 20: [(17, 1), (15, 3)], 21: [(18, 2)], 23: [(10, 3), (17, 2)], 25: [(11, 3), (18, 3)], 27: [(17, 3)]},
    {1: [(4, 0), (5, 0), (4, 1), (1, 0), (6, 0), (5, 1), (4, 2), (5, 2), (4, 3), (1, 1), (6, 1), (5, 3), (2, 0), (3, 0), (7, 0), (1, 2), (6, 2), (12, 0), (7, 1), (12, 1), (7, 2), (1, 3), (6, 3), (12, 2)], 2: [(7, 3), (12, 3)], 4: [(2, 1), (8, 0), (3, 1), (2, 2), (10, 0), (13, 0), (2, 3), (8, 1)], 6: [(10, 1), (13, 1)], 8: [(8, 2), (9, 0)], 10: [(3, 2), (13, 2), (14, 0)], 12: [(8, 3), (10, 2), (9, 1)], 14: [(13, 3), (14, 1)], 15: [(16, 0), (9, 2), (19, 0)], 16: [(11, 0), (14, 2), (15, 0), (16, 1), (9, 3)], 17: [(19, 1), (11, 1), (14, 3)], 18: [(15, 1)], 19: [(16, 2), (19, 2), (18, 0), (11, 2), (17, 0), (15, 2), (16, 3), (3, 3)], 20: [(19, 3), (18, 1)], 21: [(10, 3), (17, 1), (15, 3)], 23: [(18, 2)], 25: [(17, 2)], 27: [(11, 3), (18, 3)], 29: [(17, 3)]},
)
lag = 3
ring = 12

group_total = len(groups)
pieces = 4
moves = ((1, 0, 0), (3, 0, 0), (0, 1, 0), (0, 3, 0), (0, 0, 1), (0, 0, 3))
numbers = []
for group in groups:
    numbers.append(tuple(range(sum(map(len, numbers)), sum(map(len, numbers)) + len(group))))
first_group = {}
for index, group in enumerate(groups):
    for r, _ in group:
        first_group.setdefault(r, index)
step_total = sum(map(len, groups))


def kernel(x_ref, y_ref, gx_ref, gy_ref, held, total, weight_sum, norm_col, norm_row, stage, rho, own_d, other_d,
           out_part, in_part, out_sum, in_sum, mean_row, sum_col, land,
           got_sem, sent_sem, half_sem, d_sent, d_got, part_sent, part_got, sum_sent, sum_got, land_sem):
    half, width = x_ref.shape
    block = 2 * half
    piece = block // pieces
    gx, gy = lax.axis_index("gx"), lax.axis_index("gy")
    px, pz_hi = gx // 2, gx % 2
    py, pz_lo, core = gy // 4, (gy // 2) % 2, gy % 2
    pz = pz_hi * 2 + pz_lo
    factor = math.sqrt(width) / (block * 64)

    def place(move):
        cx, cy, cz = (px + move[0]) % 4, (py + move[1]) % 4, (pz + move[2]) % 4
        return (cx * 2 + cz // 2, (cy * 2 + cz % 2) * 2 + core)

    near = [place(move) for move in moves]
    partner = (gx, gy + 1 - 2 * core)

    def piece_rows(q):
        side = core if q < pieces // 2 else 1 - core
        return pl.ds(pl.multiple_of(side * half + (q % (pieces // 2)) * piece, piece), piece)

    def block_copy(parent, child, q, gen):
        return pltpu.make_async_remote_copy(
            src_ref=held.at[parent, piece_rows(q)],
            dst_ref=held.at[child, piece_rows(q)],
            send_sem=sent_sem.at[child, q],
            recv_sem=got_sem.at[child, q],
            device_id=near[gen ^ 1],
            device_id_type=MESH,
        )

    def half_copy():
        rows = pl.ds(pl.multiple_of(core * half, half), half)
        return pltpu.make_async_remote_copy(
            src_ref=stage, dst_ref=held.at[0, rows], send_sem=half_sem.at[0], recv_sem=half_sem.at[1],
            device_id=partner, device_id_type=MESH,
        )

    def d_copy(slot):
        return pltpu.make_async_remote_copy(
            src_ref=own_d.at[slot], dst_ref=other_d.at[slot], send_sem=d_sent.at[slot], recv_sem=d_got.at[slot],
            device_id=partner, device_id_type=MESH,
        )

    def part_copy(r, q):
        rows = pl.ds(q * piece, piece)
        return pltpu.make_async_remote_copy(
            src_ref=out_part.at[r - 1, rows], dst_ref=in_part.at[r - 1, rows],
            send_sem=part_sent.at[r - 1, q], recv_sem=part_got.at[r - 1, q],
            device_id=near[row_gen[r]], device_id_type=MESH,
        )

    def sum_copy(r):
        return pltpu.make_async_remote_copy(
            src_ref=out_sum.at[r - 1], dst_ref=in_sum.at[r - 1],
            send_sem=sum_sent.at[r - 1], recv_sem=sum_got.at[r - 1],
            device_id=near[row_gen[r]], device_id_type=MESH,
        )

    first = core == 0
    own_rows = pl.ds(pl.multiple_of(core * half, half), half)
    held[0, own_rows] = jnp.where(first, x_ref[...], y_ref[...])
    stage[...] = jnp.where(first, y_ref[...], x_ref[...])

    barrier = pltpu.get_barrier_semaphore()
    for other in [partner] + near:
        pl.semaphore_signal(barrier, inc=1, device_id=other, device_id_type=MESH)
    pl.semaphore_wait(barrier, 7)

    half_copy().start()

    def send_on(c, slot, q):
        for child in kids[c][slot]:
            block_copy(slot, child, q, slot_gen[c][child]).start()

    def event(c, slot, q):
        parent = slot_parent[c][slot]
        block_copy(parent, slot, q, slot_gen[c][slot]).wait_recv()
        send_on(c, slot, q)

    def on_core(c, events):
        @pl.when(core == c)
        def _():
            for slot, q in events:
                event(c, slot, q)

    for c in (0, 1):

        @pl.when(core == c)
        def _(c=c):
            for q in range(pieces // 2):
                send_on(c, 0, q)

    half_copy().wait()

    for c in (0, 1):

        @pl.when(core == c)
        def _(c=c):
            for q in range(pieces // 2, pieces):
                send_on(c, 0, q)

    def norms(slot):
        wide = held[slot].astype(jnp.float32)
        square = wide * wide
        part = square[:, 0:128]
        for col in range(128, width, 128):
            part = part + square[:, col : col + 128]
        turned = jnp.sum(jnp.transpose(part), axis=0, keepdims=True) + dist_eps
        norm_row[slot] = jnp.broadcast_to(turned, (8, block))
        if slot < row_total:
            norm_col[slot] = jnp.broadcast_to(jnp.sum(part, axis=1, keepdims=True), (block, 128))
            mean = jnp.sum(wide, axis=0, keepdims=True) * (1.0 / block)
            mean_row[slot] = jnp.broadcast_to(mean, (8, width))

    def stage_a(k, r, t):
        slot = k % ring
        gram = lax.dot_general(held[r], held[t], (((1,), (1,)), ((), ())), preferred_element_type=jnp.float32)
        left = jnp.concatenate([norm_col[r]] * (block // 128), axis=1)
        square = (left + norm_row[t][0:1, :]) - 2.0 * gram
        square = jnp.maximum(square, 1e-20)
        inverse = lax.rsqrt(square)
        rho[slot] = inverse
        own_d[slot] = square * inverse

    def stage_b(index):
        rows_here = sorted({r for r, _ in groups[index]})
        for r in rows_here:
            new = first_group[r] == index
            value = None if new else total[r]
            sums = None if new else weight_sum[r]
            for k, (row, t) in zip(numbers[index], groups[index]):
                if row != r:
                    continue
                slot = k % ring
                weight = (1.0 - other_d[slot] * rho[slot]).astype(jnp.bfloat16)
                term = jnp.dot(weight, held[t], preferred_element_type=jnp.float32)
                value = term if value is None else value + term
                wide = weight.astype(jnp.float32)
                for col in range(0, block, 128):
                    part = wide[:, col : col + 128]
                    sums = part if sums is None else sums + part
            total[r] = value
            weight_sum[r] = sums

    def row_sums(r):
        sums = jnp.sum(weight_sum[r], axis=1, keepdims=True)
        sum_col[r] = jnp.broadcast_to(sums, (block, 128))

    def kids_of(r):
        return [s for s in range(row_total) if row_parent[s] == r]

    def finish_wait(r):
        for s in kids_of(r):
            sum_copy(s).wait_recv()
            for q in range(pieces):
                part_copy(s, q).wait_recv()

    def finish_compute(r):
        row_sums(r)
        sums = jnp.transpose(sum_col[r])[0:8, :]
        for s in kids_of(r):
            sums = sums + in_sum[s - 1]
        out_sum[r - 1] = sums
        for q in range(pieces):
            rows = pl.ds(q * piece, piece)
            scale = jnp.concatenate([sum_col[r, rows]] * (width // 128), axis=1)
            value = total[r, rows] - scale * mean_row[r, 0:1, :]
            for s in kids_of(r):
                value = value + in_part[s - 1, rows].astype(jnp.float32)
            out_part[r - 1, rows] = value.astype(jnp.bfloat16)

    def finish_send(r):
        sum_copy(r).start()
        for q in range(pieces):
            part_copy(r, q).start()

    for index in range(group_total + lag):
        for c in (0, 1):
            if index in events[c]:
                on_core(c, events[c][index])
        back = index - lag
        done = finish_at.get(index, ())
        for r in done:
            finish_wait(r)
        if back >= 0:
            for k in numbers[back]:
                d_copy(k % ring).wait_recv()
        if index < group_total:
            for k in numbers[index]:
                if k >= ring:
                    d_copy(k % ring).wait_send()
        for slot in sorted(first_use):
            if first_use[slot] == index:
                norms(slot)
        if index < group_total:
            for k, (r, t) in zip(numbers[index], groups[index]):
                stage_a(k, r, t)
        if back >= 0:
            stage_b(back)
        for r in done:
            finish_compute(r)
        if index < group_total:
            for k in numbers[index]:
                d_copy(k % ring).start()
        for r in done:
            finish_send(r)
    for r in finish_at.get(group_total + lag, ()):
        finish_wait(r)
        finish_compute(r)
        finish_send(r)

    row_sums(0)
    sums = jnp.transpose(sum_col[0])[0:8, :]
    for s in kids_of(0):
        sum_copy(s).wait_recv()
        sums = sums + in_sum[s - 1]
    norm_col[0] = jnp.transpose(jnp.concatenate([sums] * 16, axis=0))
    for s in kids_of(0):
        for q in range(pieces):
            part_copy(s, q).wait_recv()

    def final_rows(place_to, side):
        for i in range(half // piece):
            rows = pl.ds(pl.multiple_of(side * half + i * piece, piece), piece)
            own_scale = jnp.concatenate([sum_col[0, rows]] * (width // 128), axis=1)
            scale = jnp.concatenate([norm_col[0, rows]] * (width // 128), axis=1)
            mean = mean_row[0, 0:1, :]
            value = total[0, rows] - own_scale * mean
            for s in kids_of(0):
                value = value + in_part[s - 1, rows].astype(jnp.float32)
            here = pl.ds(i * piece, piece)
            land[place_to, here] = factor * (scale * (held[0, rows].astype(jnp.float32) - mean) - value)

    def land_copy():
        return pltpu.make_async_remote_copy(
            src_ref=land.at[0], dst_ref=land.at[1], send_sem=land_sem.at[0], recv_sem=land_sem.at[1],
            device_id=partner, device_id_type=MESH,
        )

    final_rows(0, 1 - core)
    land_copy().start()
    final_rows(2, core)

    for c in (0, 1):

        @pl.when(core == c)
        def _(c=c):
            for child in range(1, slot_total):
                for q in range(pieces):
                    block_copy(slot_parent[c][child], child, q, slot_gen[c][child]).wait_send()

    for r in range(1, row_total):
        sum_copy(r).wait_send()
        for q in range(pieces):
            part_copy(r, q).wait_send()
    for slot in range(ring):
        d_copy(slot).wait_send()
    land_copy().wait()
    gx_ref[...] = jnp.where(first, land[2], land[1])
    gy_ref[...] = jnp.where(first, land[1], land[2])


def per_device(x_embed, y_embed):
    half, width = x_embed.shape
    block = 2 * half
    out = jax.ShapeDtypeStruct((half, width), jnp.float32)
    dma = pltpu.SemaphoreType.DMA
    return pl.pallas_call(
        kernel,
        out_shape=(out, out),
        in_specs=[pl.BlockSpec(memory_space=pltpu.VMEM)] * 2,
        out_specs=[pl.BlockSpec(memory_space=pltpu.VMEM)] * 2,
        scratch_shapes=[
            pltpu.VMEM((slot_total, block, width), jnp.bfloat16),
            pltpu.VMEM((row_total, block, width), jnp.float32),
            pltpu.VMEM((row_total, block, 128), jnp.float32),
            pltpu.VMEM((row_total, block, 128), jnp.float32),
            pltpu.VMEM((slot_total, 8, block), jnp.float32),
            pltpu.VMEM((half, width), jnp.bfloat16),
            pltpu.VMEM((ring, block, block), jnp.float32),
            pltpu.VMEM((ring, block, block), jnp.float32),
            pltpu.VMEM((ring, block, block), jnp.float32),
            pltpu.VMEM((row_total - 1, block, width), jnp.bfloat16),
            pltpu.VMEM((row_total - 1, block, width), jnp.bfloat16),
            pltpu.VMEM((row_total - 1, 8, block), jnp.float32),
            pltpu.VMEM((row_total - 1, 8, block), jnp.float32),
            pltpu.VMEM((row_total, 8, width), jnp.float32),
            pltpu.VMEM((row_total, block, 128), jnp.float32),
            pltpu.VMEM((3, half, width), jnp.float32),
            dma((slot_total, pieces)),
            dma((slot_total, pieces)),
            dma((2,)),
            dma((ring,)),
            dma((ring,)),
            dma((row_total - 1, pieces)),
            dma((row_total - 1, pieces)),
            dma((row_total - 1,)),
            dma((row_total - 1,)),
            dma((2,)),
        ],
        compiler_params=pltpu.CompilerParams(
            collective_id=0, has_side_effects=True, vmem_limit_bytes=56 * 2**20
        ),
        cost_estimate=pl.CostEstimate(
            flops=4 * step_total * block * block * width,
            bytes_accessed=12 * half * width,
            transcendentals=step_total * block * block,
        ),
        name="relational",
    )(x_embed, y_embed)


def solution(mesh):
    spec = P(("gx", "gy"), None)
    return jax.shard_map(
        per_device, mesh=mesh, in_specs=(spec, spec), out_specs=(spec, spec), check_vma=False
    )
```

```python
import functools
import math

import jax
import jax.numpy as jnp
from jax import lax
from jax.experimental import pallas as pl
from jax.experimental.pallas import tpu as pltpu
from jax.sharding import PartitionSpec as P

MESH = pl.DeviceIdType.MESH
dist_eps = 0.0001

slot_offsets = ((0, 0, 0), (3, 0, 0), (0, 1, 0), (1, 0, 0), (0, 3, 0), (0, 0, 1), (0, 0, 3), (2, 0, 0), (0, 2, 0), (1, 2, 0), (3, 2, 0), (2, 0, 1), (2, 1, 1), (2, 3, 1), (0, 0, 2), (2, 1, 2), (2, 2, 2), (0, 3, 2), (3, 0, 3), (1, 2, 3), (2, 2, 3))
slot_total = 21
row_total = 7
row_parent = (-1, 0, 0, 0, 0, 0, 0)
row_gen = (-1, 1, 2, 0, 3, 4, 5)
slot_parent = ((-1, 0, 0, 0, 0, 0, 0, 1, 2, 8, 8, 7, 11, 11, 6, 12, 20, 14, 6, 9, 19), (-1, 0, 0, 0, 0, 0, 0, 3, 2, 8, 8, 7, 11, 11, 5, 12, 15, 14, 1, 9, 19))
slot_gen = ((-1, 1, 2, 0, 3, 4, 5, 1, 2, 0, 1, 4, 2, 3, 5, 4, 5, 3, 1, 5, 0), (-1, 1, 2, 0, 3, 4, 5, 0, 2, 0, 1, 4, 2, 3, 4, 4, 2, 3, 5, 5, 0))
kids = (((2, 1, 6, 3, 4, 5), (7,), (8,), (), (), (), (14, 18), (11,), (9, 10), (19,), (), (12, 13), (15,), (), (17,), (), (), (), (), (20,), (16,)), ((3, 2, 5, 1, 4, 6), (18,), (8,), (7,), (), (14,), (), (11,), (9, 10), (19,), (), (12, 13), (15,), (), (17,), (16,), (), (), (), (20,), ()))
groups = (((0, 0),), ((0, 2),), ((3, 2), (5, 2)), ((5, 3), (2, 1)), ((2, 6), (2, 3)), ((2, 5), (6, 1)), ((6, 3), (4, 3)), ((4, 5), (0, 1)), ((0, 6), (0, 3)), ((0, 4), (0, 5)), ((3, 14), (4, 14)), ((1, 14), (0, 14)), ((2, 7), (5, 7)), ((4, 7), (0, 7)), ((5, 8), (2, 18)), ((4, 18), (6, 8)), ((0, 8), (0, 18)), ((6, 9), (1, 9)), ((6, 11), (0, 9)), ((2, 17), (3, 17)), ((1, 17), (0, 11)), ((0, 17),), ((4, 12), (3, 12)), ((2, 19), (5, 10)), ((5, 19), (4, 19)), ((6, 10), (1, 12)), ((0, 12), (0, 10)), ((0, 19),), ((6, 13), (3, 13)), ((4, 20), (6, 15)), ((3, 15), (1, 13)), ((1, 15), (0, 13)), ((1, 16), (0, 20)), ((0, 15), (0, 16)))
first_use = {0: 0, 2: 1, 3: 2, 5: 2, 1: 3, 6: 4, 4: 6, 14: 10, 7: 12, 8: 14, 18: 14, 9: 17, 11: 18, 17: 19, 12: 22, 19: 23, 10: 23, 13: 28, 20: 29, 15: 29, 16: 32}
finish_at = {28: [2], 29: [5], 34: [4, 6], 35: [3], 37: [1]}
events = (
    {1: [(2, 0), (1, 0), (6, 0), (3, 0), (4, 0), (5, 0), (2, 1), (1, 1), (6, 1), (3, 1), (4, 1), (5, 1), (2, 2), (1, 2), (6, 2), (3, 2), (4, 2), (5, 2), (2, 3), (1, 3), (6, 3), (3, 3), (4, 3), (5, 3)], 5: [(8, 0), (7, 0), (14, 0)], 7: [(8, 1), (18, 0), (14, 1)], 8: [(7, 1)], 10: [(18, 1), (17, 0), (8, 2), (7, 2), (14, 2), (9, 0), (11, 0), (8, 3), (18, 2), (14, 3)], 11: [(9, 1)], 12: [(17, 1), (7, 3)], 14: [(18, 3), (11, 1)], 15: [(12, 0), (10, 0), (19, 0), (9, 2)], 17: [(10, 1), (19, 1), (9, 3), (17, 2), (11, 2), (13, 0), (12, 1)], 18: [(11, 3)], 19: [(17, 3), (10, 2), (19, 2), (20, 0), (15, 0)], 21: [(10, 3), (19, 3), (20, 1)], 22: [(12, 2), (13, 1), (12, 3)], 23: [(15, 1)], 24: [(16, 0), (20, 2)], 26: [(16, 1), (20, 3)], 27: [(13, 2)], 28: [(15, 2), (13, 3)], 29: [(15, 3)], 30: [(16, 2)], 32: [(16, 3)]},
    {1: [(2, 0), (1, 0), (6, 0), (3, 0), (4, 0), (5, 0), (2, 1), (1, 1), (6, 1), (3, 1), (4, 1), (5, 1), (2, 2), (1, 2), (6, 2), (3, 2), (4, 2), (5, 2), (2, 3)], 2: [(1, 3), (6, 3), (3, 3), (4, 3), (5, 3)], 5: [(7, 0), (14, 0)], 7: [(7, 1), (14, 1)], 8: [(8, 0), (18, 0), (7, 2), (14, 2)], 10: [(8, 1), (18, 1), (7, 3), (14, 3), (17, 0)], 11: [(11, 0)], 12: [(8, 2), (18, 2), (9, 0), (11, 1)], 13: [(17, 1)], 14: [(8, 3), (18, 3), (9, 1)], 15: [(17, 2), (11, 2)], 16: [(17, 3)], 17: [(12, 0), (11, 3), (12, 1), (10, 0), (19, 0), (9, 2), (10, 1), (19, 1), (9, 3)], 19: [(12, 2)], 20: [(13, 0)], 21: [(12, 3), (15, 0)], 22: [(13, 1), (10, 2), (19, 2), (20, 0), (15, 1)], 23: [(10, 3), (19, 3), (20, 1)], 24: [(13, 2), (15, 2)], 25: [(13, 3), (16, 0)], 26: [(15, 3)], 27: [(16, 1)], 28: [(20, 2)], 29: [(20, 3)], 30: [(16, 2)], 32: [(16, 3)]},
)
lag = 4
ring = 16

group_total = len(groups)
pieces = 4
moves = ((1, 0, 0), (3, 0, 0), (0, 1, 0), (0, 3, 0), (0, 0, 1), (0, 0, 3))
numbers = []
for group in groups:
    numbers.append(tuple(range(sum(map(len, numbers)), sum(map(len, numbers)) + len(group))))
first_group = {}
for index, group in enumerate(groups):
    for r, _ in group:
        first_group.setdefault(r, index)
step_total = sum(map(len, groups))


def kernel(x_ref, y_ref, gx_ref, gy_ref, held, total, weight_sum, norm_col, norm_row, stage, rho, own_d, other_d,
           out_part, in_part, out_sum, in_sum, mean_row, sum_col, land,
           got_sem, sent_sem, half_sem, d_sent, d_got, part_sent, part_got, sum_sent, sum_got, land_sem):
    half, width = x_ref.shape
    block = 2 * half
    piece = block // pieces
    gx, gy = lax.axis_index("gx"), lax.axis_index("gy")
    px, pz_hi = gx // 2, gx % 2
    py, pz_lo, core = gy // 4, (gy // 2) % 2, gy % 2
    pz = pz_hi * 2 + pz_lo
    factor = math.sqrt(width) / (block * 64)

    def place(move):
        cx, cy, cz = (px + move[0]) % 4, (py + move[1]) % 4, (pz + move[2]) % 4
        return (cx * 2 + cz // 2, (cy * 2 + cz % 2) * 2 + core)

    near = [place(move) for move in moves]
    partner = (gx, gy + 1 - 2 * core)

    def piece_rows(q):
        side = core if q < pieces // 2 else 1 - core
        return pl.ds(pl.multiple_of(side * half + (q % (pieces // 2)) * piece, piece), piece)

    def block_copy(parent, child, q, gen):
        return pltpu.make_async_remote_copy(
            src_ref=held.at[parent, piece_rows(q)],
            dst_ref=held.at[child, piece_rows(q)],
            send_sem=sent_sem.at[child, q],
            recv_sem=got_sem.at[child, q],
            device_id=near[gen ^ 1],
            device_id_type=MESH,
        )

    def half_copy():
        rows = pl.ds(pl.multiple_of(core * half, half), half)
        return pltpu.make_async_remote_copy(
            src_ref=stage, dst_ref=held.at[0, rows], send_sem=half_sem.at[0], recv_sem=half_sem.at[1],
            device_id=partner, device_id_type=MESH,
        )

    def d_copy(slot):
        return pltpu.make_async_remote_copy(
            src_ref=own_d.at[slot], dst_ref=other_d.at[slot], send_sem=d_sent.at[slot], recv_sem=d_got.at[slot],
            device_id=partner, device_id_type=MESH,
        )

    def part_copy(r, q):
        rows = pl.ds(q * piece, piece)
        return pltpu.make_async_remote_copy(
            src_ref=out_part.at[r - 1, rows], dst_ref=in_part.at[r - 1, rows],
            send_sem=part_sent.at[r - 1, q], recv_sem=part_got.at[r - 1, q],
            device_id=near[row_gen[r]], device_id_type=MESH,
        )

    def sum_copy(r):
        return pltpu.make_async_remote_copy(
            src_ref=out_sum.at[r - 1], dst_ref=in_sum.at[r - 1],
            send_sem=sum_sent.at[r - 1], recv_sem=sum_got.at[r - 1],
            device_id=near[row_gen[r]], device_id_type=MESH,
        )

    first = core == 0
    own_rows = pl.ds(pl.multiple_of(core * half, half), half)
    held[0, own_rows] = jnp.where(first, x_ref[...], y_ref[...])
    stage[...] = jnp.where(first, y_ref[...], x_ref[...])

    barrier = pltpu.get_barrier_semaphore()
    for other in [partner] + near:
        pl.semaphore_signal(barrier, inc=1, device_id=other, device_id_type=MESH)
    pl.semaphore_wait(barrier, 7)

    half_copy().start()

    def send_on(c, slot, q):
        for child in kids[c][slot]:
            block_copy(slot, child, q, slot_gen[c][child]).start()

    def event(c, slot, q):
        parent = slot_parent[c][slot]
        block_copy(parent, slot, q, slot_gen[c][slot]).wait_recv()
        send_on(c, slot, q)

    def on_core(c, events):
        @pl.when(core == c)
        def _():
            for slot, q in events:
                event(c, slot, q)

    for c in (0, 1):

        @pl.when(core == c)
        def _(c=c):
            for q in range(pieces // 2):
                send_on(c, 0, q)

    half_copy().wait()

    for c in (0, 1):

        @pl.when(core == c)
        def _(c=c):
            for q in range(pieces // 2, pieces):
                send_on(c, 0, q)

    def norms(slot):
        wide = held[slot].astype(jnp.float32)
        square = wide * wide
        part = square[:, 0:128]
        for col in range(128, width, 128):
            part = part + square[:, col : col + 128]
        turned = jnp.sum(jnp.transpose(part), axis=0, keepdims=True) + dist_eps
        norm_row[slot] = jnp.broadcast_to(turned, (8, block))
        if slot < row_total:
            norm_col[slot] = jnp.broadcast_to(jnp.sum(part, axis=1, keepdims=True), (block, 128))
            mean = jnp.sum(wide, axis=0, keepdims=True) * (1.0 / block)
            mean_row[slot] = jnp.broadcast_to(mean, (8, width))

    def stage_a(k, r, t):
        slot = k % ring
        gram = lax.dot_general(held[r], held[t], (((1,), (1,)), ((), ())), preferred_element_type=jnp.float32)
        left = jnp.concatenate([norm_col[r]] * (block // 128), axis=1)
        square = (left + norm_row[t][0:1, :]) - 2.0 * gram
        square = jnp.maximum(square, 1e-20)
        inverse = lax.rsqrt(square)
        rho[slot] = inverse
        own_d[slot] = square * inverse

    def stage_b(index):
        rows_here = sorted({r for r, _ in groups[index]})
        for r in rows_here:
            new = first_group[r] == index
            value = None if new else total[r]
            sums = None if new else weight_sum[r]
            for k, (row, t) in zip(numbers[index], groups[index]):
                if row != r:
                    continue
                slot = k % ring
                weight = (1.0 - other_d[slot] * rho[slot]).astype(jnp.bfloat16)
                term = jnp.dot(weight, held[t], preferred_element_type=jnp.float32)
                value = term if value is None else value + term
                wide = weight.astype(jnp.float32)
                for col in range(0, block, 128):
                    part = wide[:, col : col + 128]
                    sums = part if sums is None else sums + part
            total[r] = value
            weight_sum[r] = sums

    def row_sums(r):
        sums = jnp.sum(weight_sum[r], axis=1, keepdims=True)
        sum_col[r] = jnp.broadcast_to(sums, (block, 128))

    def kids_of(r):
        return [s for s in range(row_total) if row_parent[s] == r]

    def finish_wait(r):
        for s in kids_of(r):
            sum_copy(s).wait_recv()
            for q in range(pieces):
                part_copy(s, q).wait_recv()

    def finish_compute(r):
        row_sums(r)
        sums = jnp.transpose(sum_col[r])[0:8, :]
        for s in kids_of(r):
            sums = sums + in_sum[s - 1]
        out_sum[r - 1] = sums
        for q in range(pieces):
            rows = pl.ds(q * piece, piece)
            scale = jnp.concatenate([sum_col[r, rows]] * (width // 128), axis=1)
            value = total[r, rows] - scale * mean_row[r, 0:1, :]
            for s in kids_of(r):
                value = value + in_part[s - 1, rows].astype(jnp.float32)
            out_part[r - 1, rows] = value.astype(jnp.bfloat16)

    def finish_send(r):
        sum_copy(r).start()
        for q in range(pieces):
            part_copy(r, q).start()

    for index in range(group_total + lag):
        for c in (0, 1):
            if index in events[c]:
                on_core(c, events[c][index])
        back = index - lag
        done = finish_at.get(index, ())
        for r in done:
            finish_wait(r)
        if back >= 0:
            for k in numbers[back]:
                d_copy(k % ring).wait_recv()
        if index < group_total:
            for k in numbers[index]:
                if k >= ring:
                    d_copy(k % ring).wait_send()
        for slot in sorted(first_use):
            if first_use[slot] == index:
                norms(slot)
        if index < group_total:
            for k, (r, t) in zip(numbers[index], groups[index]):
                stage_a(k, r, t)
        if back >= 0:
            stage_b(back)
        for r in done:
            finish_compute(r)
        if index < group_total:
            for k in numbers[index]:
                d_copy(k % ring).start()
        for r in done:
            finish_send(r)
    for r in finish_at.get(group_total + lag, ()):
        finish_wait(r)
        finish_compute(r)
        finish_send(r)

    row_sums(0)
    sums = jnp.transpose(sum_col[0])[0:8, :]
    for s in kids_of(0):
        sum_copy(s).wait_recv()
        sums = sums + in_sum[s - 1]
    norm_col[0] = jnp.transpose(jnp.concatenate([sums] * 16, axis=0))
    for s in kids_of(0):
        for q in range(pieces):
            part_copy(s, q).wait_recv()

    def final_rows(place_to, side):
        for i in range(half // piece):
            rows = pl.ds(pl.multiple_of(side * half + i * piece, piece), piece)
            own_scale = jnp.concatenate([sum_col[0, rows]] * (width // 128), axis=1)
            scale = jnp.concatenate([norm_col[0, rows]] * (width // 128), axis=1)
            mean = mean_row[0, 0:1, :]
            value = total[0, rows] - own_scale * mean
            for s in kids_of(0):
                value = value + in_part[s - 1, rows].astype(jnp.float32)
            here = pl.ds(i * piece, piece)
            land[place_to, here] = factor * (scale * (held[0, rows].astype(jnp.float32) - mean) - value)

    def land_copy():
        return pltpu.make_async_remote_copy(
            src_ref=land.at[0], dst_ref=land.at[1], send_sem=land_sem.at[0], recv_sem=land_sem.at[1],
            device_id=partner, device_id_type=MESH,
        )

    final_rows(0, 1 - core)
    land_copy().start()
    final_rows(2, core)

    for c in (0, 1):

        @pl.when(core == c)
        def _(c=c):
            for child in range(1, slot_total):
                for q in range(pieces):
                    block_copy(slot_parent[c][child], child, q, slot_gen[c][child]).wait_send()

    for r in range(1, row_total):
        sum_copy(r).wait_send()
        for q in range(pieces):
            part_copy(r, q).wait_send()
    for slot in range(ring):
        d_copy(slot).wait_send()
    land_copy().wait()
    gx_ref[...] = jnp.where(first, land[2], land[1])
    gy_ref[...] = jnp.where(first, land[1], land[2])


def per_device(x_embed, y_embed):
    half, width = x_embed.shape
    block = 2 * half
    out = jax.ShapeDtypeStruct((half, width), jnp.float32)
    dma = pltpu.SemaphoreType.DMA
    return pl.pallas_call(
        kernel,
        out_shape=(out, out),
        in_specs=[pl.BlockSpec(memory_space=pltpu.VMEM)] * 2,
        out_specs=[pl.BlockSpec(memory_space=pltpu.VMEM)] * 2,
        scratch_shapes=[
            pltpu.VMEM((slot_total, block, width), jnp.bfloat16),
            pltpu.VMEM((row_total, block, width), jnp.float32),
            pltpu.VMEM((row_total, block, 128), jnp.float32),
            pltpu.VMEM((row_total, block, 128), jnp.float32),
            pltpu.VMEM((slot_total, 8, block), jnp.float32),
            pltpu.VMEM((half, width), jnp.bfloat16),
            pltpu.VMEM((ring, block, block), jnp.float32),
            pltpu.VMEM((ring, block, block), jnp.float32),
            pltpu.VMEM((ring, block, block), jnp.float32),
            pltpu.VMEM((row_total - 1, block, width), jnp.bfloat16),
            pltpu.VMEM((row_total - 1, block, width), jnp.bfloat16),
            pltpu.VMEM((row_total - 1, 8, block), jnp.float32),
            pltpu.VMEM((row_total - 1, 8, block), jnp.float32),
            pltpu.VMEM((row_total, 8, width), jnp.float32),
            pltpu.VMEM((row_total, block, 128), jnp.float32),
            pltpu.VMEM((3, half, width), jnp.float32),
            dma((slot_total, pieces)),
            dma((slot_total, pieces)),
            dma((2,)),
            dma((ring,)),
            dma((ring,)),
            dma((row_total - 1, pieces)),
            dma((row_total - 1, pieces)),
            dma((row_total - 1,)),
            dma((row_total - 1,)),
            dma((2,)),
        ],
        compiler_params=pltpu.CompilerParams(
            collective_id=0, has_side_effects=True, vmem_limit_bytes=56 * 2**20
        ),
        cost_estimate=pl.CostEstimate(
            flops=4 * step_total * block * block * width,
            bytes_accessed=12 * half * width,
            transcendentals=step_total * block * block,
        ),
        name="relational",
    )(x_embed, y_embed)


def solution(mesh):
    spec = P(("gx", "gy"), None)
    return jax.shard_map(
        per_device, mesh=mesh, in_specs=(spec, spec), out_specs=(spec, spec), check_vma=False
    )
```

```python
import functools
import math

import jax
import jax.numpy as jnp
from jax import lax
from jax.experimental import pallas as pl
from jax.experimental.pallas import tpu as pltpu
from jax.sharding import PartitionSpec as P

MESH = pl.DeviceIdType.MESH
dist_eps = 0.0001

slot_offsets = ((0, 0, 0), (3, 0, 0), (0, 1, 0), (1, 0, 0), (0, 3, 0), (0, 0, 1), (0, 0, 3), (2, 0, 0), (0, 2, 0), (1, 2, 0), (3, 2, 0), (2, 0, 1), (2, 1, 1), (2, 3, 1), (0, 0, 2), (2, 1, 2), (2, 2, 2), (0, 3, 2), (3, 0, 3), (1, 2, 3), (2, 2, 3))
slot_total = 21
row_total = 7
row_parent = (-1, 0, 0, 0, 0, 0, 0)
row_gen = (-1, 1, 2, 0, 3, 4, 5)
slot_parent = ((-1, 0, 0, 0, 0, 0, 0, 1, 2, 8, 8, 7, 11, 11, 6, 12, 20, 14, 6, 9, 19), (-1, 0, 0, 0, 0, 0, 0, 3, 2, 8, 8, 7, 11, 11, 5, 12, 15, 14, 1, 9, 19))
slot_gen = ((-1, 1, 2, 0, 3, 4, 5, 1, 2, 0, 1, 4, 2, 3, 5, 4, 5, 3, 1, 5, 0), (-1, 1, 2, 0, 3, 4, 5, 0, 2, 0, 1, 4, 2, 3, 4, 4, 2, 3, 5, 5, 0))
kids = (((2, 1, 6, 3, 4, 5), (7,), (8,), (), (), (), (14, 18), (11,), (9, 10), (19,), (), (12, 13), (15,), (), (17,), (), (), (), (), (20,), (16,)), ((3, 2, 5, 1, 4, 6), (18,), (8,), (7,), (), (14,), (), (11,), (9, 10), (19,), (), (12, 13), (15,), (), (17,), (16,), (), (), (), (20,), ()))
groups = (((0, 0),), ((0, 2),), ((3, 2), (5, 2)), ((5, 3), (2, 1)), ((2, 6), (2, 3)), ((2, 5), (6, 1)), ((6, 3), (4, 3)), ((4, 5), (0, 1)), ((0, 6), (0, 3)), ((0, 4), (0, 5)), ((3, 14), (4, 14)), ((1, 14), (0, 14)), ((2, 7), (5, 7)), ((4, 7), (0, 7)), ((5, 8), (2, 18)), ((4, 18), (6, 8)), ((0, 8), (0, 18)), ((6, 9), (1, 9)), ((6, 11), (0, 9)), ((2, 17), (3, 17)), ((1, 17), (0, 11)), ((0, 17),), ((4, 12), (3, 12)), ((2, 19), (5, 10)), ((5, 19), (4, 19)), ((6, 10), (1, 12)), ((0, 12), (0, 10)), ((0, 19),), ((6, 13), (3, 13)), ((4, 20), (6, 15)), ((3, 15), (1, 13)), ((1, 15), (0, 13)), ((1, 16), (0, 20)), ((0, 15), (0, 16)))
first_use = {0: 0, 2: 1, 3: 2, 5: 2, 1: 3, 6: 4, 4: 6, 14: 10, 7: 12, 8: 14, 18: 14, 9: 17, 11: 18, 17: 19, 12: 22, 19: 23, 10: 23, 13: 28, 20: 29, 15: 29, 16: 32}
finish_at = {28: [2], 29: [5], 34: [4, 6], 35: [3], 37: [1]}
events = (
    {1: [(2, 0), (1, 0), (6, 0), (3, 0), (4, 0), (5, 0), (2, 1), (1, 1), (6, 1), (3, 1), (4, 1), (5, 1), (2, 2), (1, 2), (6, 2), (3, 2), (4, 2), (5, 2), (2, 3), (1, 3), (6, 3), (3, 3), (4, 3), (5, 3)], 5: [(8, 0), (7, 0), (14, 0)], 7: [(8, 1), (18, 0), (14, 1)], 8: [(7, 1)], 10: [(18, 1), (17, 0), (8, 2), (7, 2), (14, 2), (9, 0), (11, 0), (8, 3), (18, 2), (14, 3)], 11: [(9, 1)], 12: [(17, 1), (7, 3)], 14: [(18, 3), (11, 1)], 15: [(12, 0), (10, 0), (19, 0), (9, 2)], 17: [(10, 1), (19, 1), (9, 3), (17, 2), (11, 2), (13, 0), (12, 1)], 18: [(11, 3)], 19: [(17, 3), (10, 2), (19, 2), (20, 0), (15, 0)], 21: [(10, 3), (19, 3), (20, 1)], 22: [(12, 2), (13, 1), (12, 3)], 23: [(15, 1)], 24: [(16, 0), (20, 2)], 26: [(16, 1), (20, 3)], 27: [(13, 2)], 28: [(15, 2), (13, 3)], 29: [(15, 3)], 30: [(16, 2)], 32: [(16, 3)]},
    {1: [(2, 0), (1, 0), (6, 0), (3, 0), (4, 0), (5, 0), (2, 1), (1, 1), (6, 1), (3, 1), (4, 1), (5, 1), (2, 2), (1, 2), (6, 2), (3, 2), (4, 2), (5, 2), (2, 3)], 2: [(1, 3), (6, 3), (3, 3), (4, 3), (5, 3)], 5: [(7, 0), (14, 0)], 7: [(7, 1), (14, 1)], 8: [(8, 0), (18, 0), (7, 2), (14, 2)], 10: [(8, 1), (18, 1), (7, 3), (14, 3), (17, 0)], 11: [(11, 0)], 12: [(8, 2), (18, 2), (9, 0), (11, 1)], 13: [(17, 1)], 14: [(8, 3), (18, 3), (9, 1)], 15: [(17, 2), (11, 2)], 16: [(17, 3)], 17: [(12, 0), (11, 3), (12, 1), (10, 0), (19, 0), (9, 2), (10, 1), (19, 1), (9, 3)], 19: [(12, 2)], 20: [(13, 0)], 21: [(12, 3), (15, 0)], 22: [(13, 1), (10, 2), (19, 2), (20, 0), (15, 1)], 23: [(10, 3), (19, 3), (20, 1)], 24: [(13, 2), (15, 2)], 25: [(13, 3), (16, 0)], 26: [(15, 3)], 27: [(16, 1)], 28: [(20, 2)], 29: [(20, 3)], 30: [(16, 2)], 32: [(16, 3)]},
)
lag = 4
ring = 16

group_total = len(groups)
pieces = 4
moves = ((1, 0, 0), (3, 0, 0), (0, 1, 0), (0, 3, 0), (0, 0, 1), (0, 0, 3))
numbers = []
for group in groups:
    numbers.append(tuple(range(sum(map(len, numbers)), sum(map(len, numbers)) + len(group))))
first_group = {}
for index, group in enumerate(groups):
    for r, _ in group:
        first_group.setdefault(r, index)
step_total = sum(map(len, groups))


def kernel(x_ref, y_ref, gx_ref, gy_ref, held, total, weight_sum, norm_col, norm_row, stage, rho, own_d, other_d,
           out_part, in_part, out_sum, in_sum, mean_row, sum_col, land,
           got_sem, sent_sem, half_sem, d_sent, d_got, part_sent, part_got, sum_sent, sum_got, land_sem):
    half, width = x_ref.shape
    block = 2 * half
    piece = block // pieces
    gx, gy = lax.axis_index("gx"), lax.axis_index("gy")
    px, pz_hi = gx // 2, gx % 2
    py, pz_lo, core = gy // 4, (gy // 2) % 2, gy % 2
    pz = pz_hi * 2 + pz_lo
    factor = math.sqrt(width) / (block * 64)

    def place(move):
        cx, cy, cz = (px + move[0]) % 4, (py + move[1]) % 4, (pz + move[2]) % 4
        return (cx * 2 + cz // 2, (cy * 2 + cz % 2) * 2 + core)

    near = [place(move) for move in moves]
    partner = (gx, gy + 1 - 2 * core)

    def piece_rows(q):
        side = core if q < pieces // 2 else 1 - core
        return pl.ds(pl.multiple_of(side * half + (q % (pieces // 2)) * piece, piece), piece)

    def block_copy(parent, child, q, gen):
        return pltpu.make_async_remote_copy(
            src_ref=held.at[parent, piece_rows(q)],
            dst_ref=held.at[child, piece_rows(q)],
            send_sem=sent_sem.at[child, q],
            recv_sem=got_sem.at[child, q],
            device_id=near[gen ^ 1],
            device_id_type=MESH,
        )

    def half_copy():
        rows = pl.ds(pl.multiple_of(core * half, half), half)
        return pltpu.make_async_remote_copy(
            src_ref=stage, dst_ref=held.at[0, rows], send_sem=half_sem.at[0], recv_sem=half_sem.at[1],
            device_id=partner, device_id_type=MESH,
        )

    def d_copy(slot):
        return pltpu.make_async_remote_copy(
            src_ref=own_d.at[slot], dst_ref=other_d.at[slot], send_sem=d_sent.at[slot], recv_sem=d_got.at[slot],
            device_id=partner, device_id_type=MESH,
        )

    def part_copy(r, q):
        side = 1 - core if q < pieces // 2 else core
        rows = pl.ds(pl.multiple_of(side * half + (q % (pieces // 2)) * piece, piece), piece)
        return pltpu.make_async_remote_copy(
            src_ref=out_part.at[r - 1, rows], dst_ref=in_part.at[r - 1, rows],
            send_sem=part_sent.at[r - 1, q], recv_sem=part_got.at[r - 1, q],
            device_id=near[row_gen[r]], device_id_type=MESH,
        )

    def sum_copy(r):
        return pltpu.make_async_remote_copy(
            src_ref=out_sum.at[r - 1], dst_ref=in_sum.at[r - 1],
            send_sem=sum_sent.at[r - 1], recv_sem=sum_got.at[r - 1],
            device_id=near[row_gen[r]], device_id_type=MESH,
        )

    first = core == 0
    own_rows = pl.ds(pl.multiple_of(core * half, half), half)
    held[0, own_rows] = jnp.where(first, x_ref[...], y_ref[...])
    stage[...] = jnp.where(first, y_ref[...], x_ref[...])

    barrier = pltpu.get_barrier_semaphore()
    for other in [partner] + near:
        pl.semaphore_signal(barrier, inc=1, device_id=other, device_id_type=MESH)
    pl.semaphore_wait(barrier, 7)

    half_copy().start()

    def send_on(c, slot, q):
        for child in kids[c][slot]:
            block_copy(slot, child, q, slot_gen[c][child]).start()

    def event(c, slot, q):
        parent = slot_parent[c][slot]
        block_copy(parent, slot, q, slot_gen[c][slot]).wait_recv()
        send_on(c, slot, q)

    def on_core(c, events):
        @pl.when(core == c)
        def _():
            for slot, q in events:
                event(c, slot, q)

    for c in (0, 1):

        @pl.when(core == c)
        def _(c=c):
            for q in range(pieces // 2):
                send_on(c, 0, q)

    half_copy().wait()

    for c in (0, 1):

        @pl.when(core == c)
        def _(c=c):
            for q in range(pieces // 2, pieces):
                send_on(c, 0, q)

    def norms(slot):
        wide = held[slot].astype(jnp.float32)
        square = wide * wide
        part = square[:, 0:128]
        for col in range(128, width, 128):
            part = part + square[:, col : col + 128]
        turned = jnp.sum(jnp.transpose(part), axis=0, keepdims=True) + dist_eps
        norm_row[slot] = jnp.broadcast_to(turned, (8, block))
        if slot < row_total:
            norm_col[slot] = jnp.broadcast_to(jnp.sum(part, axis=1, keepdims=True), (block, 128))
            mean = jnp.sum(wide, axis=0, keepdims=True) * (1.0 / block)
            mean_row[slot] = jnp.broadcast_to(mean, (8, width))

    def stage_a(k, r, t):
        slot = k % ring
        gram = lax.dot_general(held[r], held[t], (((1,), (1,)), ((), ())), preferred_element_type=jnp.float32)
        left = jnp.concatenate([norm_col[r]] * (block // 128), axis=1)
        square = (left + norm_row[t][0:1, :]) - 2.0 * gram
        square = jnp.maximum(square, 1e-20)
        inverse = lax.rsqrt(square)
        rho[slot] = inverse
        own_d[slot] = square * inverse

    def stage_b(index):
        rows_here = sorted({r for r, _ in groups[index]})
        for r in rows_here:
            new = first_group[r] == index
            value = None if new else total[r]
            sums = None if new else weight_sum[r]
            for k, (row, t) in zip(numbers[index], groups[index]):
                if row != r:
                    continue
                slot = k % ring
                weight = (1.0 - other_d[slot] * rho[slot]).astype(jnp.bfloat16)
                term = jnp.dot(weight, held[t], preferred_element_type=jnp.float32)
                value = term if value is None else value + term
                wide = weight.astype(jnp.float32)
                for col in range(0, block, 128):
                    part = wide[:, col : col + 128]
                    sums = part if sums is None else sums + part
            total[r] = value
            weight_sum[r] = sums

    def row_sums(r):
        sums = jnp.sum(weight_sum[r], axis=1, keepdims=True)
        sum_col[r] = jnp.broadcast_to(sums, (block, 128))

    def kids_of(r):
        return [s for s in range(row_total) if row_parent[s] == r]

    def finish_wait(r):
        for s in kids_of(r):
            sum_copy(s).wait_recv()
            for q in range(pieces):
                part_copy(s, q).wait_recv()

    def finish_compute(r):
        row_sums(r)
        sums = jnp.transpose(sum_col[r])[0:8, :]
        for s in kids_of(r):
            sums = sums + in_sum[s - 1]
        out_sum[r - 1] = sums
        for q in range(pieces):
            rows = pl.ds(q * piece, piece)
            scale = jnp.concatenate([sum_col[r, rows]] * (width // 128), axis=1)
            value = total[r, rows] - scale * mean_row[r, 0:1, :]
            for s in kids_of(r):
                value = value + in_part[s - 1, rows].astype(jnp.float32)
            out_part[r - 1, rows] = value.astype(jnp.bfloat16)

    def finish_send(r):
        sum_copy(r).start()
        for q in range(pieces):
            part_copy(r, q).start()

    for index in range(group_total + lag):
        for c in (0, 1):
            if index in events[c]:
                on_core(c, events[c][index])
        back = index - lag
        done = finish_at.get(index, ())
        for r in done:
            finish_wait(r)
        if back >= 0:
            for k in numbers[back]:
                d_copy(k % ring).wait_recv()
        if index < group_total:
            for k in numbers[index]:
                if k >= ring:
                    d_copy(k % ring).wait_send()
        for slot in sorted(first_use):
            if first_use[slot] == index:
                norms(slot)
        if index < group_total:
            for k, (r, t) in zip(numbers[index], groups[index]):
                stage_a(k, r, t)
        if back >= 0:
            stage_b(back)
        for r in done:
            finish_compute(r)
        if index < group_total:
            for k in numbers[index]:
                d_copy(k % ring).start()
        for r in done:
            finish_send(r)
    for r in finish_at.get(group_total + lag, ()):
        finish_wait(r)
        finish_compute(r)
        finish_send(r)

    row_sums(0)
    sums = jnp.transpose(sum_col[0])[0:8, :]
    for s in kids_of(0):
        sum_copy(s).wait_recv()
        sums = sums + in_sum[s - 1]
    norm_col[0] = jnp.transpose(jnp.concatenate([sums] * 16, axis=0))
    def final_rows(place_to, side):
        for i in range(half // piece):
            rows = pl.ds(pl.multiple_of(side * half + i * piece, piece), piece)
            own_scale = jnp.concatenate([sum_col[0, rows]] * (width // 128), axis=1)
            scale = jnp.concatenate([norm_col[0, rows]] * (width // 128), axis=1)
            mean = mean_row[0, 0:1, :]
            value = total[0, rows] - own_scale * mean
            for s in kids_of(0):
                value = value + in_part[s - 1, rows].astype(jnp.float32)
            here = pl.ds(i * piece, piece)
            land[place_to, here] = factor * (scale * (held[0, rows].astype(jnp.float32) - mean) - value)

    def land_copy():
        return pltpu.make_async_remote_copy(
            src_ref=land.at[0], dst_ref=land.at[1], send_sem=land_sem.at[0], recv_sem=land_sem.at[1],
            device_id=partner, device_id_type=MESH,
        )

    for s in kids_of(0):
        for q in range(pieces // 2):
            part_copy(s, q).wait_recv()
    final_rows(0, 1 - core)
    land_copy().start()
    for s in kids_of(0):
        for q in range(pieces // 2, pieces):
            part_copy(s, q).wait_recv()
    final_rows(2, core)

    for c in (0, 1):

        @pl.when(core == c)
        def _(c=c):
            for child in range(1, slot_total):
                for q in range(pieces):
                    block_copy(slot_parent[c][child], child, q, slot_gen[c][child]).wait_send()

    for r in range(1, row_total):
        sum_copy(r).wait_send()
        for q in range(pieces):
            part_copy(r, q).wait_send()
    for slot in range(ring):
        d_copy(slot).wait_send()
    land_copy().wait()
    gx_ref[...] = jnp.where(first, land[2], land[1])
    gy_ref[...] = jnp.where(first, land[1], land[2])


def per_device(x_embed, y_embed):
    half, width = x_embed.shape
    block = 2 * half
    out = jax.ShapeDtypeStruct((half, width), jnp.float32)
    dma = pltpu.SemaphoreType.DMA
    return pl.pallas_call(
        kernel,
        out_shape=(out, out),
        in_specs=[pl.BlockSpec(memory_space=pltpu.VMEM)] * 2,
        out_specs=[pl.BlockSpec(memory_space=pltpu.VMEM)] * 2,
        scratch_shapes=[
            pltpu.VMEM((slot_total, block, width), jnp.bfloat16),
            pltpu.VMEM((row_total, block, width), jnp.float32),
            pltpu.VMEM((row_total, block, 128), jnp.float32),
            pltpu.VMEM((row_total, block, 128), jnp.float32),
            pltpu.VMEM((slot_total, 8, block), jnp.float32),
            pltpu.VMEM((half, width), jnp.bfloat16),
            pltpu.VMEM((ring, block, block), jnp.float32),
            pltpu.VMEM((ring, block, block), jnp.float32),
            pltpu.VMEM((ring, block, block), jnp.float32),
            pltpu.VMEM((row_total - 1, block, width), jnp.bfloat16),
            pltpu.VMEM((row_total - 1, block, width), jnp.bfloat16),
            pltpu.VMEM((row_total - 1, 8, block), jnp.float32),
            pltpu.VMEM((row_total - 1, 8, block), jnp.float32),
            pltpu.VMEM((row_total, 8, width), jnp.float32),
            pltpu.VMEM((row_total, block, 128), jnp.float32),
            pltpu.VMEM((3, half, width), jnp.float32),
            dma((slot_total, pieces)),
            dma((slot_total, pieces)),
            dma((2,)),
            dma((ring,)),
            dma((ring,)),
            dma((row_total - 1, pieces)),
            dma((row_total - 1, pieces)),
            dma((row_total - 1,)),
            dma((row_total - 1,)),
            dma((2,)),
        ],
        compiler_params=pltpu.CompilerParams(
            collective_id=0, has_side_effects=True, vmem_limit_bytes=56 * 2**20
        ),
        cost_estimate=pl.CostEstimate(
            flops=4 * step_total * block * block * width,
            bytes_accessed=12 * half * width,
            transcendentals=step_total * block * block,
        ),
        name="relational",
    )(x_embed, y_embed)


def solution(mesh):
    spec = P(("gx", "gy"), None)
    return jax.shard_map(
        per_device, mesh=mesh, in_specs=(spec, spec), out_specs=(spec, spec), check_vma=False
    )
```
